32 devices in a mesh: batch: 8 (over z, x), tensor: 4 (over y, core).
Axes of the slice: x: 2, y: 2, z: 4, core: 2. Of those that a mesh axis runs over, the one named last changes fastest.
Arguments:
- tokens: bfloat16 [16384, 768], P(('batch', 'tensor')), may hold values from -6 to 6
- source_subset: int32 [8], P('batch'), may hold values from 0 to 21
- subset_weight: float32 [22], replicated, may hold values from 0.25 to 4
- output_cotangent: bfloat16 [16384, 768], P(('batch', 'tensor')), may hold values from -6 to 6
- attention_gain: float32 [768], replicated, may hold values from 0.25 to 1.75
- attention_shift: float32 [768], replicated, may hold values from -3 to 3
- feed_gain: float32 [768], replicated, may hold values from 0.25 to 1.75
- feed_shift: float32 [768], replicated, may hold values from -3 to 3
- query_weight: bfloat16 [768, 768], P(None, 'tensor'), may hold values from -0.21875 to 0.21875
- query_bias: bfloat16 [768], P('tensor'), may hold values from -3 to 3
- shared_weight: bfloat16 [768, 128], replicated, may hold values from -0.21875 to 0.21875
- shared_bias: bfloat16 [128], replicated, may hold values from -3 to 3
- out_weight: bfloat16 [768, 768], P(None, 'tensor'), may hold values from -1.5 to 1.5
- up_weight: bfloat16 [768, 3072], P(None, 'tensor'), may hold values from -0.21875 to 0.21875
- up_bias: bfloat16 [3072], P('tensor'), may hold values from -3 to 3
- down_weight: bfloat16 [768, 3072], P(None, 'tensor'), may hold values from -0.109375 to 0.109375
- out_bias: bfloat16 [768], replicated, may hold values from -3 to 3
Outputs:
- mixed: bfloat16 [16384, 768], P(('batch', 'tensor'))
- tokens_gradient: bfloat16 [16384, 768], P(('batch', 'tensor'))
- attention_gain_gradient: float32 [768], replicated
- attention_shift_gradient: float32 [768], replicated
- feed_gain_gradient: float32 [768], replicated
- feed_shift_gradient: float32 [768], replicated
- query_weight_gradient: float32 [768, 768], P(None, 'tensor')
- query_bias_gradient: float32 [768], P('tensor')
- shared_weight_gradient: float32 [768, 128], replicated
- shared_bias_gradient: float32 [128], replicated
- out_weight_gradient: float32 [768, 768], P(None, 'tensor')
- up_weight_gradient: float32 [768, 3072], P(None, 'tensor')
- up_bias_gradient: float32 [3072], P('tensor')
- down_weight_gradient: float32 [768, 3072], P(None, 'tensor')
- out_bias_gradient: float32 [768], replicated
The draws below stay inside these ranges and needn't reach their ends.
All inputs are finite; a program needn't handle non-finite values.
Results may differ from the reference program's by a relative error of at most 0.012.
The reference program's roundings to bfloat16 on the way count: a program that leaves them out, or rounds other values in their place, can miss the bound.
Values may be sent and summed in bfloat16 or wider, within the bound.
No kernel may reach another device: no remote copies, remote signals or barrier semaphores. Data moves between devices by JAX's collectives and lax.ppermute only.
A program may use at most 128 MiB of HBM per device.

```python
import math
import jax
import jax.numpy as jnp
import numpy as np
from jax import lax

D = 768
HEADS = 12
HEAD_DIM = 64
FF = 3072
LEN = 2048
SEQS = 1
SUBSETS = 22
ROT = 16
SEQUENCES = 8
TOKENS = 16384
N_BATCH = 8


def set_ends(drawn, key, smallest, top_value):
    place = [jax.random.randint(jax.random.fold_in(key, axis), (), 0, length) for axis, length in enumerate(drawn.shape)]
    main_axis = drawn.shape.index(max(drawn.shape))
    next_to = place[:main_axis] + [(place[main_axis] + 1) % drawn.shape[main_axis]] + place[main_axis + 1:]
    return drawn.at[tuple(place)].set(smallest).at[tuple(next_to)].set(top_value)


def shard_levels(key, dims, cuts, low, largest):
    loudness = 1.0
    for position, blocks in cuts:
        steps = jax.random.uniform(jax.random.fold_in(jax.random.fold_in(key, 6), position), (blocks,), jnp.float32, low / len(cuts), largest / len(cuts))
        loudness = loudness * jnp.repeat(jnp.exp(steps), dims[position] // blocks).reshape((-1,) + (1,) * (len(dims) - 1 - position))
    return loudness


def cumulative_ranks(count, lean):
    loads = [(1 << 20) // math.isqrt(standing ** lean) + 1 for standing in range(1, count + 1)]
    deviation = 1 + sum(loads) // (1 << 30)
    return np.cumsum(np.array([max(1, weight // deviation) for weight in loads]))


def skewed_ids(own_key, shape, number_of, skew):
    listing = cumulative_ranks(number_of, skew)
    pick = jax.random.randint(jax.random.fold_in(own_key, 1), shape, 0, int(listing[number_of - 1]))
    grade = jnp.searchsorted(jnp.asarray(listing, jnp.int32), pick, side="right")
    return jax.random.permutation(jax.random.fold_in(own_key, 2), number_of)[grade].astype(jnp.int32)


def noise(own_key, dims, spread, reach, cuts=(), kind=jnp.bfloat16):
    values = spread * jax.random.normal(own_key, dims, jnp.float32)
    if cuts:
        values = values * shard_levels(own_key, dims, cuts, -0.22, 0.18)
    return jnp.clip(values, -reach, reach).astype(kind)


def setup_inputs(seed: int = 0) -> dict:
    arg_keys = jax.random.split(jax.random.key(seed), 18)
    return {
        "tokens": noise(arg_keys[0], (TOKENS, D), 1.0, 6.0, ((0, 32),)),
        "source_subset": set_ends(skewed_ids(arg_keys[1], (SEQUENCES,), SUBSETS, 2), jax.random.fold_in(arg_keys[1], 3), 0, SUBSETS - 1).astype(jnp.int32),
        "subset_weight": jnp.clip(jnp.exp(jax.random.uniform(arg_keys[2], (SUBSETS,), jnp.float32, math.log(0.25), math.log(4.0))), 0.25, 4.0),
        "output_cotangent": noise(arg_keys[3], (TOKENS, D), 1.0, 6.0, ((0, 32),)),
        "attention_gain": jnp.clip(1.0 + 0.15 * jax.random.normal(arg_keys[4], (D,), jnp.float32), 0.25, 1.75),
        "attention_shift": noise(arg_keys[5], (D,), 0.5, 3.0, (), jnp.float32),
        "feed_gain": jnp.clip(1.0 + 0.15 * jax.random.normal(arg_keys[6], (D,), jnp.float32), 0.25, 1.75),
        "feed_shift": noise(arg_keys[7], (D,), 0.5, 3.0, (), jnp.float32),
        "query_weight": noise(arg_keys[8], (D, HEADS * HEAD_DIM), D ** -0.5, 0.21875, ((1, 4),)),
        "query_bias": noise(arg_keys[9], (HEADS * HEAD_DIM,), 0.5, 3.0, ((0, 4),)),
        "shared_weight": noise(arg_keys[10], (D, 2 * HEAD_DIM), D ** -0.5, 0.21875),
        "shared_bias": noise(arg_keys[11], (2 * HEAD_DIM,), 0.5, 3.0),
        "out_weight": noise(arg_keys[12], (D, HEADS * HEAD_DIM), 16 ** -0.5, 1.5, ((1, 4),)),
        "up_weight": noise(arg_keys[13], (D, FF), D ** -0.5, 0.21875, ((1, 4),)),
        "up_bias": noise(arg_keys[14], (FF,), 0.5, 3.0, ((0, 4),)),
        "down_weight": noise(arg_keys[15], (D, FF), FF ** -0.5, 0.109375, ((1, 4),)),
        "out_bias": noise(arg_keys[16], (D,), 0.5, 3.0),
    }


EPSILON = 1e-05
NEGATIVE = -1e+30
HIGHEST = lax.Precision.HIGHEST

@jax.custom_vjp
def low(v):
    return lax.optimization_barrier(v.astype(jnp.bfloat16)).astype(jnp.float32)

@jax.custom_vjp
def low_back(v):
    return v

def low_keep(v):
    return (low(v), None)

def low_pass(kept, grad):
    return (grad,)

def back_keep(v):
    return (v, None)

def back_low(kept, grad):
    return (low(grad),)
low.defvjp(low_keep, low_pass)
low_back.defvjp(back_keep, back_low)

def layer_norm(values, gain, shift):
    centred = values - lax.optimization_barrier(jnp.mean(values, axis=-1, keepdims=True))
    variance = lax.optimization_barrier(jnp.mean(centred * centred, axis=-1, keepdims=True))
    return centred * lax.rsqrt(variance + EPSILON) * gain + shift

def rotary_tables(positions):
    half = ROT // 2
    frequency = 10000.0 ** (-2.0 * jnp.arange(half, dtype=jnp.float32) / ROT)
    angles = positions.astype(jnp.float32)[:, None] * frequency[None, :]
    angles = jnp.concatenate([angles, angles], axis=1)
    return (jnp.cos(angles), jnp.sin(angles))

def rotate(values, cosine, sine):
    half = ROT // 2
    turned = values[..., :ROT]
    swapped = jnp.concatenate([-turned[..., half:], turned[..., :half]], axis=-1)
    return jnp.concatenate([turned * cosine + swapped * sine, values[..., ROT:]], axis=-1)

def attend_group(queries, keys, values):
    block = min(512, LEN)
    scale = HEAD_DIM ** (-0.5)

    def one_block(index):
        start = index * block
        sequence_start = start // LEN * LEN
        query_block = lax.dynamic_slice_in_dim(queries, start, block, 1)
        key_block = lax.dynamic_slice_in_dim(keys, sequence_start, LEN, 0)
        value_block = lax.dynamic_slice_in_dim(values, sequence_start, LEN, 0)
        scores = low_back(jnp.einsum('hqd,kd->hqk', query_block, key_block, precision=HIGHEST) * scale)
        places = start - sequence_start + jnp.arange(block, dtype=jnp.int32)
        allowed = jnp.arange(LEN, dtype=jnp.int32)[None, :] <= places[:, None]
        scores = jnp.where(allowed[None], scores, NEGATIVE)
        soft = low(jax.nn.softmax(scores, axis=-1))
        return jnp.einsum('hqk,kd->hqd', soft, value_block, precision=HIGHEST)
    return lax.map(jax.checkpoint(one_block), jnp.arange(queries.shape[1] // block, dtype=jnp.int32))

def group_forward(tokens, attention_gain, attention_shift, feed_gain, feed_shift, query_weight, query_bias, shared_weight, shared_bias, out_weight, up_weight, up_bias, down_weight, out_bias):
    rows = tokens.shape[0]
    attention_in = low(layer_norm(tokens, attention_gain, attention_shift))
    feed_in = low(layer_norm(tokens, feed_gain, feed_shift))
    query_raw = low_back(jnp.dot(attention_in, query_weight, precision=HIGHEST) + query_bias)
    shared_raw = low_back(jnp.dot(attention_in, shared_weight, precision=HIGHEST) + shared_bias)
    cosine, sine = rotary_tables(jnp.arange(rows, dtype=jnp.int32) % LEN)
    queries = low(rotate(query_raw.reshape(rows, HEADS, HEAD_DIM).transpose(1, 0, 2), cosine, sine))
    keys = low(rotate(shared_raw[:, :HEAD_DIM], cosine, sine))
    values = low(shared_raw[:, HEAD_DIM:])
    mixed_blocks = attend_group(queries, keys, values)
    context = mixed_blocks.transpose(0, 2, 1, 3).reshape(rows, HEADS * HEAD_DIM)
    context = low(low_back(context))
    hidden_raw = low_back(jnp.dot(feed_in, up_weight, precision=HIGHEST) + up_bias)
    activated = low(jax.nn.gelu(hidden_raw, approximate=False))
    branch = jnp.dot(context, out_weight.T, precision=HIGHEST) + jnp.dot(activated, down_weight.T, precision=HIGHEST)
    return tokens + low_back(branch) + out_bias

def reference(tokens, source_subset, subset_weight, output_cotangent, attention_gain, attention_shift, feed_gain, feed_shift, query_weight, query_bias, shared_weight, shared_bias, out_weight, up_weight, up_bias, down_weight, out_bias):
    params = tuple((entry.astype(jnp.float32) for entry in (attention_gain, attention_shift, feed_gain, feed_shift, query_weight, query_bias, shared_weight, shared_bias, out_weight, up_weight, up_bias, down_weight, out_bias)))
    group_rows = SEQS * LEN
    sequence_scale = subset_weight[source_subset]
    row_scale = jnp.repeat(sequence_scale, LEN)
    outer = output_cotangent.astype(jnp.float32) * row_scale[:, None]
    token_groups = tokens.astype(jnp.float32).reshape(N_BATCH, group_rows, D)
    outer_groups = outer.reshape(N_BATCH, group_rows, D)

    def group_step(totals, pair):
        group_tokens, group_outer = pair
        result, pullback = jax.vjp(group_forward, group_tokens, *params)
        gradients = pullback(group_outer)
        totals = tuple((first + second for first, second in zip(totals, gradients[1:])))
        return (totals, (result.astype(jnp.bfloat16), gradients[0].astype(jnp.bfloat16)))
    zeros = tuple((jnp.zeros_like(entry) for entry in params))
    totals, (mixed, tokens_back) = lax.scan(group_step, zeros, (token_groups, outer_groups))
    return (mixed.reshape(N_BATCH * group_rows, D), tokens_back.reshape(N_BATCH * group_rows, D), totals[0], totals[1], totals[2], totals[3], totals[4], totals[5], totals[6], totals[7], totals[8], totals[9], totals[10], totals[11], totals[12])
```

```python
import functools

import jax
import jax.numpy as jnp
import numpy as np
from jax import lax
from jax.experimental import pallas as pl
from jax.experimental.pallas import tpu as pltpu
from jax.sharding import PartitionSpec as P

HEAD_DIM = 64
LEN = 2048
ROT = 16
HALF = ROT // 2
TILE = 256
KEYS = 512
LANES = 128

EPSILON = 1e-05
NEGATIVE = -1e30
BF = jnp.bfloat16
F32 = jnp.float32


def mm(left, right):
    return jnp.dot(left, right, preferred_element_type=F32)


def mm_rows(left, right):
    return lax.dot_general(left, right, (((0,), (0,)), ((), ())), preferred_element_type=F32)


def mm_cols(left, right):
    return lax.dot_general(left, right, (((1,), (1,)), ((), ())), preferred_element_type=F32)


def rope_tables():
    lane = np.arange(LANES) % HEAD_DIM
    frequency = (10000.0 ** (-2.0 * np.arange(HALF, dtype=np.float32) / ROT)).astype(np.float32)
    angles = np.arange(LEN, dtype=np.float32)[:, None] * frequency[lane % HALF][None, :]
    angles = angles.astype(np.float32).astype(np.float64)
    turned = lane < ROT
    cosine = np.where(turned, np.cos(angles), 1.0)
    low = np.where(lane < HALF, -np.sin(angles), 0.0)
    high = np.where((lane >= HALF) & turned, np.sin(angles), 0.0)
    return [jnp.asarray(t.astype(np.float32)) for t in (cosine, low, high)]


def turn(values, cosine, low, high, sign):
    up = pltpu.roll(values, LANES - HALF, 1)
    down = pltpu.roll(values, HALF, 1)
    return values * cosine + sign * (up * low + down * high)


def normalize(rows):
    centred = rows - jnp.mean(rows, axis=-1, keepdims=True)
    variance = jnp.mean(centred * centred, axis=-1, keepdims=True)
    scale = lax.rsqrt(variance + EPSILON)
    return centred * scale, scale


def rows_kernel(n_parts, tiles, carried, place, scale, *refs):
    tokens = refs[:n_parts]
    cots = refs[n_parts : 2 * n_parts]
    refs = refs[2 * n_parts :]
    vec, qkv_bias, cosine, low, high, w_qkv, w_up, w_down, w_out = refs[:9]
    refs = refs[9:]
    if carried:
        sums_in, vecs_in = refs[:2]
        refs = refs[2 + 8 :]
    sums, vecs, branch, feed_w, qq, kk, vv, dd, xh, ob, x_scr, g_scr = refs
    step = pl.program_id(0)
    width = w_up.shape[0]

    @pl.when(step == 0)
    def _():
        if carried:
            sums[...] = sums_in[...]
            vecs[...] = vecs_in[...]
        else:
            sums[...] = jnp.zeros_like(sums)
            vecs[...] = jnp.zeros_like(vecs)

    if n_parts > 1:
        for part in range(n_parts):

            @pl.when(step // tiles == part)
            def _(part=part):
                x_scr[...] = tokens[part][...]
                g_scr[...] = cots[part][...]

        x = x_scr[...].astype(F32)
        g = g_scr[...].astype(F32)
    else:
        x = tokens[0][...].astype(F32)
        g = cots[0][...].astype(F32)

    xhat, _ = normalize(x)
    xh[...] = xhat.astype(BF)
    attention_in = (xhat * vec[0:1, :] + vec[1:2, :]).astype(BF)
    feed_in = (xhat * vec[2:3, :] + vec[3:4, :]).astype(BF)
    outer = g * scale[0, 0]
    outer_low = outer.astype(BF)
    ob[...] = outer_low
    vecs[3:4, :] += jnp.sum(outer, axis=0, keepdims=True)

    raw = mm(attention_in, w_qkv[...]) + qkv_bias[...]
    c, l, h = cosine[...], low[...], high[...]
    qq[:, :LANES] = turn(raw[:, :LANES], c, l, h, 1.0).astype(BF)
    qq[:, LANES:] = turn(raw[:, LANES : 2 * LANES], c, l, h, 1.0).astype(BF)
    kk[...] = turn(raw[:, 2 * LANES : 3 * LANES], c, l, h, 1.0).astype(BF)
    vv[...] = raw[:, 3 * LANES :].astype(BF)
    dd[...] = mm(outer_low, w_out[...]).astype(BF)

    hidden = mm(feed_in, w_up[...]) + vec[4:5, :]
    cdf = 0.5 + 0.5 * lax.erf(hidden * (0.5**0.5))
    slope = cdf + hidden * (jnp.exp(-0.5 * hidden * hidden) * (2.0 * np.pi) ** -0.5)
    activated = (hidden * cdf).astype(BF)
    hidden_back = (mm(outer_low, w_down[...]) * slope).astype(BF)
    branch[...] = mm_cols(activated, w_down[...]).astype(BF)
    feed_back = mm_cols(hidden_back, w_up[...])
    sums[:width, :] += mm_rows(outer_low, activated)
    sums[width:, :] += mm_rows(feed_in, hidden_back)
    vecs[0:1, :] += jnp.sum(xhat * feed_back, axis=0, keepdims=True)
    vecs[1:2, :] += jnp.sum(feed_back, axis=0, keepdims=True)
    vecs[2:3, :] += jnp.sum(hidden_back.astype(F32), axis=0, keepdims=True)
    feed_w[...] = (feed_back * vec[2:3, :]).astype(BF)


def rows_call(tokens, cots, place, scale, fixed, group_rows, carried=None):
    n_parts = len(tokens)
    tiles = tokens[0].shape[0] // TILE
    width = tokens[0].shape[1]
    hidden = fixed["w_up"].shape[1]

    def part_spec(part):
        return pl.BlockSpec(
            (TILE, width), lambda i, place: (jnp.clip(i - part * tiles, 0, tiles - 1), 0)
        )

    def whole(a):
        return pl.BlockSpec(a.shape, lambda i, place: (0,) * a.ndim)

    def placed(columns):
        return pl.BlockSpec((TILE, columns), lambda i, place: (place[i], 0))

    small = [fixed["vec"], fixed["qkv_bias"]]
    tables = fixed["tables"]
    weights = [fixed["w_qkv"], fixed["w_up"], fixed["w_down"], fixed["w_out"]]
    in_specs = (
        [pl.BlockSpec(memory_space=pltpu.SMEM)]
        + [part_spec(p) for p in range(n_parts)] * 2
        + [whole(a) for a in small]
        + [placed(LANES)] * 3
        + [whole(a) for a in weights]
    )
    args = [scale, *tokens, *cots, *small, *tables, *weights]
    columns = [width, width, 2 * LANES, LANES, LANES, 2 * LANES, width, width]
    out_shape = [
        jax.ShapeDtypeStruct((2 * width, hidden), F32),
        jax.ShapeDtypeStruct((8, width), F32),
    ] + [jax.ShapeDtypeStruct((group_rows, c), BF) for c in columns]
    out_specs = [
        pl.BlockSpec((2 * width, hidden), lambda i, place: (0, 0)),
        pl.BlockSpec((8, width), lambda i, place: (0, 0)),
    ] + [placed(c) for c in columns]
    aliases = {}
    if carried is not None:
        in_specs += [whole(a) for a in carried[:2]]
        in_specs += [pl.BlockSpec(memory_space=pl.ANY)] * 8
        first = len(args) + 1
        args += list(carried)
        aliases = {first + 2 + i: 2 + i for i in range(8)}
    flops = 2 * n_parts * tiles * TILE * width * (6 * hidden + 768)
    return pl.pallas_call(
        functools.partial(rows_kernel, n_parts, tiles, carried is not None),
        grid_spec=pltpu.PrefetchScalarGridSpec(
            num_scalar_prefetch=1,
            grid=(n_parts * tiles,),
            in_specs=in_specs,
            out_specs=out_specs,
            scratch_shapes=[pltpu.VMEM((TILE, width), BF), pltpu.VMEM((TILE, width), BF)],
        ),
        out_shape=out_shape,
        input_output_aliases=aliases,
        compiler_params=pltpu.CompilerParams(vmem_limit_bytes=48 * 2**20),
        cost_estimate=pl.CostEstimate(
            flops=flops, bytes_accessed=20 * 2**20, transcendentals=0
        ),
        name="rows",
    )(place, *args)


def attention_kernel(carried, order, _rel, *refs):
    qq, dd, xh, ob, branch, feed_w, cosine, low, high = refs[:9]
    kk, vv, w_out, w_q, w_s, gain = refs[9:15]
    refs = refs[15:]
    if carried:
        ins = refs[:7]
        refs = refs[7 + 2 :]
    outs = refs[:7]
    k_sum, v_sum, g_q, g_out, g_s, b_q, b_s = outs
    branch_out, w_total, s_scr, d_scr, qt, dt, o_acc, q_acc = refs[7:]
    step = pl.program_id(0)
    block = order[step]
    heads = 3
    rows = heads * TILE

    @pl.when(step == 0)
    def _():
        for i, out in enumerate(outs):
            out[...] = ins[i][...] if carried else jnp.zeros_like(out)

    left = lax.broadcasted_iota(jnp.int32, (TILE, LANES), 1) < HEAD_DIM
    zero = jnp.zeros((TILE, LANES), BF)

    def stack(ref):
        pair, last = ref[:, :LANES], ref[:, LANES:]
        return jnp.concatenate([jnp.where(left, pair, zero), jnp.where(left, zero, pair), last], 0)

    queries = stack(qq) * jnp.asarray(HEAD_DIM**-0.5, BF)
    incoming = stack(dd)
    qt[...] = queries.T
    dt[...] = incoming.T
    n_tiles = block * TILE // KEYS + 1

    def lane_max(s):
        out = s[:, :LANES]
        for j in range(1, KEYS // LANES):
            out = jnp.maximum(out, s[:, j * LANES : (j + 1) * LANES])
        return out

    def lane_sum(s):
        out = s[:, :LANES]
        for j in range(1, KEYS // LANES):
            out = out + s[:, j * LANES : (j + 1) * LANES]
        return out

    def scores(t, peak, masked):
        at = pl.ds(pl.multiple_of(t * KEYS, KEYS), KEYS)
        s = mm_cols(queries, kk[at, :])
        if masked:
            key = t * KEYS + lax.broadcasted_iota(jnp.int32, (TILE, KEYS), 1)
            place = block * TILE + lax.broadcasted_iota(jnp.int32, (TILE, KEYS), 0)
            allowed = key <= place
            s = jnp.where(jnp.concatenate([allowed] * heads, 0), s, NEGATIVE)
        s_scr[:, at] = s
        return jnp.maximum(peak, lane_max(s))

    peak = lax.fori_loop(
        0,
        n_tiles - 1,
        lambda t, p: scores(t, p, False),
        jnp.full((rows, LANES), NEGATIVE, F32),
    )
    peak = scores(n_tiles - 1, peak, True)
    peak = jnp.max(peak, axis=1, keepdims=True)

    o_acc[...] = jnp.zeros_like(o_acc)

    def weigh(t, carry):
        total, centre = carry
        at = pl.ds(pl.multiple_of(t * KEYS, KEYS), KEYS)
        p = jnp.exp(s_scr[:, at] - peak)
        d = mm_cols(incoming, vv[at, :])
        s_scr[:, at] = p
        d_scr[:, at] = d
        o_acc[...] += mm(p.astype(BF), vv[at, :])
        return total + lane_sum(p), centre + lane_sum(p * d)

    none = jnp.zeros((rows, LANES), F32)
    total, centre = lax.fori_loop(0, n_tiles, weigh, (none, none))
    inverse = 1.0 / jnp.sum(total, axis=1, keepdims=True)
    centre = jnp.sum(centre, axis=1, keepdims=True) * inverse

    q_acc[...] = jnp.zeros_like(q_acc)

    def back(t, carry):
        at = pl.ds(pl.multiple_of(t * KEYS, KEYS), KEYS)
        p = s_scr[:, at] * inverse
        ds = (p * (d_scr[:, at] - centre)).astype(BF)
        v_sum[:, at] += mm(dt[...], p.astype(BF))
        k_sum[:, at] += mm(qt[...], ds)
        q_acc[...] += mm(ds, kk[at, :])
        return carry

    lax.fori_loop(0, n_tiles, back, 0)

    def unstack(a):
        return jnp.where(left, a[:TILE], a[TILE : 2 * TILE]), jnp.where(left, a[2 * TILE :], 0.0)

    c, l, h = cosine[...], low[...], high[...]
    mixed = o_acc[...] * inverse
    context = jnp.concatenate([a.astype(BF) for a in unstack(mixed)], 1)
    outer = ob[...]
    branch_out[...] = (
        branch[...].astype(F32) + mm_cols(context, w_out[...])
    ).astype(BF)
    g_out[...] += mm_rows(outer, context)

    turned = unstack(q_acc[...] * HEAD_DIM**-0.5)
    query_back = jnp.concatenate([turn(a, c, l, h, -1.0).astype(BF) for a in turned], 1)
    at = pl.ds(pl.multiple_of(block * TILE, TILE), TILE)
    key_back = k_sum[:, at].T
    value_back = v_sum[:, at].T
    key_back = turn(key_back + pltpu.roll(key_back, HEAD_DIM, 1), c, l, h, -1.0)
    value_back = value_back + pltpu.roll(value_back, HEAD_DIM, 1)
    shared_back = jnp.where(left, key_back, value_back).astype(BF)
    xhat = xh[...]
    g_q[...] += mm_rows(xhat, query_back)
    g_s[...] += mm_rows(xhat, shared_back)
    b_q[0:1, :] += jnp.sum(query_back.astype(F32), axis=0, keepdims=True)
    b_s[0:1, :] += jnp.sum(shared_back.astype(F32), axis=0, keepdims=True)
    e = mm_cols(query_back, w_q[...]) + mm_cols(shared_back, w_s[...])
    w_total[...] = (feed_w[...].astype(F32) + e * gain[...]).astype(BF)


def attention_call(order, rel, made, fixed, carried=None):
    branch, feed_w, qq, kk, vv, dd, xh, ob = made
    group_rows, width = xh.shape
    steps = order.shape[0]

    def placed(columns):
        return pl.BlockSpec((TILE, columns), lambda i, order, rel: (order[i], 0))

    def moved(columns):
        return pl.BlockSpec((TILE, columns), lambda i, order, rel: (rel[i], 0))

    def whole(shape):
        return pl.BlockSpec(shape, lambda i, order, rel: (0,) * len(shape))

    blocked = [qq, dd, xh, ob, branch, feed_w, *fixed["tables"]]
    full = [kk, vv, fixed["w_out"], fixed["w_q"], fixed["w_s"], fixed["gain"]]
    in_specs = [placed(a.shape[1]) for a in blocked] + [whole(a.shape) for a in full]
    args = blocked + full
    sums = [
        (LANES, group_rows),
        (LANES, group_rows),
        (width, 2 * LANES),
        (width, 2 * LANES),
        (width, LANES),
        (8, 2 * LANES),
        (8, LANES),
    ]
    out_shape = [jax.ShapeDtypeStruct(s, F32) for s in sums]
    out_shape += [jax.ShapeDtypeStruct((group_rows, width), BF)] * 2
    out_specs = [whole(s) for s in sums] + [moved(width)] * 2
    aliases = {}
    if carried is not None:
        first = len(args) + 2
        in_specs += [whole(s) for s in sums] + [pl.BlockSpec(memory_space=pl.ANY)] * 2
        args += list(carried)
        aliases = {first + 7: 7, first + 8: 8}
    rows = 3 * TILE
    return pl.pallas_call(
        functools.partial(attention_kernel, carried is not None),
        grid_spec=pltpu.PrefetchScalarGridSpec(
            num_scalar_prefetch=2,
            grid=(steps,),
            in_specs=in_specs,
            out_specs=out_specs,
            scratch_shapes=[
                pltpu.VMEM((rows, group_rows), F32),
                pltpu.VMEM((rows, group_rows), F32),
                pltpu.VMEM((LANES, rows), BF),
                pltpu.VMEM((LANES, rows), BF),
                pltpu.VMEM((rows, LANES), F32),
                pltpu.VMEM((rows, LANES), F32),
            ],
        ),
        out_shape=out_shape,
        input_output_aliases=aliases,
        compiler_params=pltpu.CompilerParams(vmem_limit_bytes=56 * 2**20),
        cost_estimate=pl.CostEstimate(
            flops=steps * 10 * 10**9, bytes_accessed=10 * 2**20, transcendentals=0
        ),
        name="attend",
    )(order, rel, *args)


def swap(a, axis, bit):
    size = lax.axis_size(axis)
    return lax.ppermute(a, axis, [(i, i ^ bit) for i in range(size)])


def bits_of(size):
    return [1 << i for i in range(size.bit_length() - 1)]


def halve(a, axis, bit):
    half = a.shape[0] // 2
    mine = (lax.axis_index(axis) // bit) % 2
    keep = lax.dynamic_slice_in_dim(a, mine * half, half, 0)
    send = lax.dynamic_slice_in_dim(a, (1 - mine) * half, half, 0)
    return keep.astype(F32) + swap(send.astype(BF), axis, bit).astype(F32)


def double(a, axis, bit):
    other = swap(a, axis, bit)
    mine = (lax.axis_index(axis) // bit) % 2
    return jnp.where(
        mine == 0, jnp.concatenate([a, other], 0), jnp.concatenate([other, a], 0)
    )


def sum_over(a, axis, order):
    for bit in order:
        a = halve(a, axis, bit)
    a = a.astype(BF)
    for bit in order[::-1]:
        a = double(a, axis, bit)
    return a


def on_device(
    tokens,
    source_subset,
    subset_weight,
    output_cotangent,
    attention_gain,
    attention_shift,
    feed_gain,
    feed_shift,
    query_weight,
    query_bias,
    shared_weight,
    shared_bias,
    out_weight,
    up_weight,
    up_bias,
    down_weight,
    out_bias,
):
    own_rows, width = tokens.shape
    parts = lax.axis_size("tensor")
    group_rows = own_rows * parts
    me = lax.axis_index("tensor")
    per = own_rows // TILE
    n_blocks = group_rows // TILE

    tok1 = swap(tokens, "tensor", 1)
    cot1 = swap(output_cotangent, "tensor", 1)
    tok2 = swap(tokens, "tensor", 2)
    cot2 = swap(output_cotangent, "tensor", 2)
    tok3 = swap(tok2, "tensor", 1)
    cot3 = swap(cot2, "tensor", 1)

    match = source_subset[0] == jnp.arange(subset_weight.shape[0], dtype=jnp.int32)
    scale = jnp.sum(jnp.where(match, subset_weight, 0.0))

    def pad(a, columns):
        return jnp.pad(a, ((0, 0), (0, columns - a.shape[1])))

    def widen(w):
        keys, values = shared_weight[:, :HEAD_DIM], shared_weight[:, HEAD_DIM:]
        return w

    local = query_weight.shape[1]
    key_part, value_part = shared_weight[:, :HEAD_DIM], shared_weight[:, HEAD_DIM:]
    w_q = pad(query_weight, 2 * LANES)
    w_qkv = jnp.concatenate([w_q, key_part, key_part, value_part, value_part], 1)
    key_bias, value_bias = shared_bias[:HEAD_DIM], shared_bias[HEAD_DIM:]
    qkv_bias = jnp.concatenate(
        [
            jnp.pad(query_bias, (0, 2 * LANES - local)),
            key_bias,
            key_bias,
            value_bias,
            value_bias,
        ]
    ).astype(F32)[None, :]
    w_out = pad(out_weight, 2 * LANES)
    zeros = jnp.zeros_like(attention_gain)
    vec = jnp.stack(
        [
            attention_gain,
            attention_shift,
            feed_gain,
            feed_shift,
            up_bias.astype(F32),
            zeros,
            zeros,
            zeros,
        ]
    )
    fixed = {
        "vec": vec,
        "qkv_bias": qkv_bias,
        "tables": rope_tables(),
        "w_qkv": w_qkv,
        "w_up": up_weight,
        "w_down": down_weight,
        "w_out": w_out,
        "w_q": w_q,
        "w_s": shared_weight,
        "gain": attention_gain[None, :],
    }

    def places(ks):
        return jnp.stack([(me ^ k) * per + h for k in ks for h in range(per)]).astype(jnp.int32)

    scale_in = scale.reshape(1, 1)
    made = rows_call(
        [tokens, tok1], [output_cotangent, cot1], places((0, 1)), scale_in, fixed, group_rows
    )
    made = rows_call(
        [tok2, tok3], [cot2, cot3], places((2, 3)), scale_in, fixed, group_rows, made
    )
    sums, vecs = made[:2]
    made = made[2:]

    bits = bits_of(lax.axis_size("batch"))
    down_sum = sum_over(sums[:width], "batch", bits)
    up_sum = sum_over(sums[width:], "batch", bits[1:] + bits[:1])

    groups = [(7,), (6,), (5,), (4, 3), (2, 1, 0)]
    carried = None
    for group in groups:
        order = jnp.asarray(np.array(group, np.int32))
        rel = ((order // per) ^ me) * per + order % per
        carried = attention_call(order, rel.astype(jnp.int32), made, fixed, carried)
    k_sum, v_sum, g_q, g_out, g_s, b_q, b_s, branch, w_total = carried

    def collect(a):
        near = a[:own_rows].astype(F32) + swap(a[own_rows : 2 * own_rows], "tensor", 1).astype(F32)
        far = a[2 * own_rows : 3 * own_rows].astype(F32) + swap(
            a[3 * own_rows :], "tensor", 1
        ).astype(F32)
        return near + swap(far.astype(BF), "tensor", 2).astype(F32)

    tokens_wide = tokens.astype(F32)
    mixed = (tokens_wide + collect(branch) + out_bias.astype(F32)).astype(BF)
    xhat, inverse = normalize(tokens_wide)
    w = collect(w_total)
    outer = output_cotangent.astype(F32) * scale
    tokens_back = outer + inverse * (
        w
        - jnp.mean(w, axis=-1, keepdims=True)
        - xhat * jnp.mean(w * xhat, axis=-1, keepdims=True)
    )
    tokens_back = tokens_back.astype(BF)

    g_q, g_out, b_q, b_s = g_q[:, :local], g_out[:, :local], b_q[0, :local], b_s[0]
    gain_back = jnp.sum(query_weight.astype(F32) * g_q, axis=1) + jnp.sum(
        shared_weight.astype(F32) * g_s, axis=1
    )
    shift_back = jnp.sum(query_weight.astype(F32) * b_q[None, :], axis=1) + jnp.sum(
        shared_weight.astype(F32) * b_s[None, :], axis=1
    )
    pair = jnp.concatenate([g_q, g_out], 1)
    pair = sum_over(pair, "batch", bits).astype(F32)
    b_q, up_back, out_back = lax.psum((b_q, vecs[2], vecs[3]), "batch")
    g_s, b_s, gain_back, shift_back, feed_gain_back, feed_shift_back = lax.psum(
        (g_s, b_s, gain_back, shift_back, vecs[0], vecs[1]), ("batch", "tensor")
    )
    query_back = pair[:, :local] * attention_gain[:, None] + attention_shift[:, None] * b_q[None, :]
    shared_back = g_s * attention_gain[:, None] + attention_shift[:, None] * b_s[None, :]
    return (
        mixed,
        tokens_back,
        gain_back,
        shift_back,
        feed_gain_back,
        feed_shift_back,
        query_back,
        b_q,
        shared_back,
        b_s,
        pair[:, local:],
        up_sum.astype(F32),
        up_back,
        down_sum.astype(F32),
        out_back,
    )


def solution(mesh):
    return jax.shard_map(
        on_device,
        mesh=mesh,
        in_specs=(
            P(("batch", "tensor"), None),
            P("batch"),
            P(),
            P(("batch", "tensor"), None),
            P(),
            P(),
            P(),
            P(),
            P(None, "tensor"),
            P("tensor"),
            P(),
            P(),
            P(None, "tensor"),
            P(None, "tensor"),
            P("tensor"),
            P(None, "tensor"),
            P(),
        ),
        out_specs=(
            P(("batch", "tensor"), None),
            P(("batch", "tensor"), None),
            P(),
            P(),
            P(),
            P(),
            P(None, "tensor"),
            P("tensor"),
            P(),
            P(),
            P(None, "tensor"),
            P(None, "tensor"),
            P("tensor"),
            P(None, "tensor"),
            P(),
        ),
        check_vma=False,
    )
```

```python
import functools

import jax
import jax.numpy as jnp
import numpy as np
from jax import lax
from jax.experimental import pallas as pl
from jax.experimental.pallas import tpu as pltpu
from jax.sharding import PartitionSpec as P

HEAD_DIM = 64
LEN = 2048
ROT = 16
HALF = ROT // 2
TILE = 512
BLOCK = 512
LANES = 128
SMALL = 192

EPSILON = 1e-05
NEGATIVE = -1e30
BF = jnp.bfloat16
F32 = jnp.float32


def mm(left, right):
    return jnp.dot(left, right, preferred_element_type=F32)


def mm_rows(left, right):
    return lax.dot_general(left, right, (((0,), (0,)), ((), ())), preferred_element_type=F32)


def mm_cols(left, right):
    return lax.dot_general(left, right, (((1,), (1,)), ((), ())), preferred_element_type=F32)


def rope_tables():
    lane = np.arange(LANES) % HEAD_DIM
    frequency = (10000.0 ** (-2.0 * np.arange(HALF, dtype=np.float32) / ROT)).astype(np.float32)
    angles = np.arange(LEN, dtype=np.float32)[:, None] * frequency[lane % HALF][None, :]
    angles = angles.astype(np.float32).astype(np.float64)
    turned = lane < ROT
    cosine = np.where(turned, np.cos(angles), 1.0)
    low = np.where(lane < HALF, -np.sin(angles), 0.0)
    high = np.where((lane >= HALF) & turned, np.sin(angles), 0.0)
    return [jnp.asarray(t.astype(np.float32)) for t in (cosine, low, high)]


def turn(values, cosine, low, high, sign):
    up = pltpu.roll(values, LANES - HALF, 1)
    down = pltpu.roll(values, HALF, 1)
    return values * cosine + sign * (up * low + down * high)


def normalize(rows):
    centred = rows - jnp.mean(rows, axis=-1, keepdims=True)
    variance = jnp.mean(centred * centred, axis=-1, keepdims=True)
    scale = lax.rsqrt(variance + EPSILON)
    return centred * scale, scale


def rows_kernel(n_parts, tiles, carried, last, place, scale, *refs):
    tokens = refs[:n_parts]
    cots = refs[n_parts : 2 * n_parts]
    refs = refs[2 * n_parts :]
    vec, qkv_bias, cosine, low, high, w_qkv, w_up, w_down, w_out = refs[:9]
    refs = refs[9:]
    if carried:
        sums_in, vecs_in = refs[:2]
        refs = refs[2 + 8 :]
    sums_out, vecs, act, back, qq, kk, vv, dd, xh, ob, x_scr, g_scr = refs[:12]
    sums = refs[12] if last else sums_out
    step = pl.program_id(0)
    width = w_up.shape[0]

    @pl.when(step == 0)
    def _():
        if carried:
            sums[...] = sums_in[...]
            vecs[...] = vecs_in[...]
        else:
            sums[...] = jnp.zeros_like(sums)
            vecs[...] = jnp.zeros_like(vecs)

    for part in range(n_parts):

        @pl.when(step // tiles == part)
        def _(part=part):
            x_scr[...] = tokens[part][...]
            g_scr[...] = cots[part][...]

    xhat, _ = normalize(x_scr[...].astype(F32))
    xhat_low = xhat.astype(BF)
    xh[...] = xhat_low
    attention_in = (xhat * vec[0:1, :] + vec[1:2, :]).astype(BF)
    feed_in = (xhat * vec[2:3, :] + vec[3:4, :]).astype(BF)
    outer = g_scr[...].astype(F32) * scale[0, 0]
    outer_low = outer.astype(BF)
    ob[...] = outer_low
    vecs[3:4, :] += jnp.sum(outer, axis=0, keepdims=True)

    hidden = mm(feed_in, w_up[...]) + vec[4:5, :]
    cdf = 0.5 + 0.5 * lax.erf(hidden * (0.5**0.5))
    slope = cdf + hidden * (jnp.exp(-0.5 * hidden * hidden) * (2.0 * np.pi) ** -0.5)
    activated = (hidden * cdf).astype(BF)
    act[...] = activated
    hidden_back = (mm(outer_low, w_down[...]) * slope).astype(BF)
    back[...] = hidden_back
    sums[:width, :] += mm_rows(outer_low, activated)
    sums[width:, :] += mm_rows(xhat_low, hidden_back)
    vecs[2:3, :] += jnp.sum(hidden_back.astype(F32), axis=0, keepdims=True)

    raw = mm(attention_in, w_qkv[...]) + qkv_bias[...]
    c, l, h = cosine[...], low[...], high[...]
    qq[:, :LANES] = turn(raw[:, :LANES], c, l, h, 1.0).astype(BF)
    qq[:, LANES:] = turn(raw[:, LANES : 2 * LANES], c, l, h, 1.0).astype(BF)
    kk[...] = turn(raw[:, 2 * LANES : 3 * LANES], c, l, h, 1.0).astype(BF)
    vv[...] = raw[:, 3 * LANES :].astype(BF)
    dd[...] = mm(outer_low, w_out[...]).astype(BF)

    if last:

        @pl.when(step == pl.num_programs(0) - 1)
        def _():
            sums_out[...] = sums[...].astype(BF)
            up = w_up[...].astype(F32)
            gain_back = jnp.sum(up * sums[width:, :], 1, keepdims=True)
            shift_back = jnp.sum(up * vecs[2:3, :], 1, keepdims=True)
            vecs[0:2, :] = as_rows(gain_back, shift_back)


def as_rows(first, second):
    lane = lax.broadcasted_iota(jnp.int32, (first.shape[0], LANES), 1)
    return jnp.where(lane == 0, first, second).T[:2, :]


def rows_call(tokens, cots, tile, place, scale, fixed, group_rows, carried=None, last=False):
    n_parts = len(tokens)
    tiles = tokens[0].shape[0] // tile
    width = tokens[0].shape[1]
    hidden = fixed["w_up"].shape[1]

    def part_spec(part):
        return pl.BlockSpec(
            (tile, width), lambda i, place: (jnp.clip(i - part * tiles, 0, tiles - 1), 0)
        )

    def whole(a):
        return pl.BlockSpec(a.shape, lambda i, place: (0,) * a.ndim)

    def placed(columns):
        return pl.BlockSpec((tile, columns), lambda i, place: (place[i], 0))

    small = [fixed["vec"], fixed["qkv_bias"]]
    tables = fixed["tables"]
    weights = [fixed["w_qkv"], fixed["w_up"], fixed["w_down"], fixed["w_out"]]
    in_specs = (
        [pl.BlockSpec(memory_space=pltpu.SMEM)]
        + [part_spec(p) for p in range(n_parts)] * 2
        + [whole(a) for a in small]
        + [placed(LANES)] * 3
        + [whole(a) for a in weights]
    )
    args = [scale, *tokens, *cots, *small, *tables, *weights]
    columns = [hidden, hidden, 2 * LANES, LANES, LANES, 2 * LANES, width, width]
    out_shape = [
        jax.ShapeDtypeStruct((2 * width, hidden), BF if last else F32),
        jax.ShapeDtypeStruct((8, width), F32),
    ] + [jax.ShapeDtypeStruct((group_rows, c), BF) for c in columns]
    out_specs = [
        pl.BlockSpec((2 * width, hidden), lambda i, place: (0, 0)),
        pl.BlockSpec((8, width), lambda i, place: (0, 0)),
    ] + [placed(c) for c in columns]
    aliases = {}
    if carried is not None:
        in_specs += [whole(a) for a in carried[:2]]
        in_specs += [pl.BlockSpec(memory_space=pl.ANY)] * 8
        first = len(args) + 1
        args += list(carried)
        aliases = {first + 2 + i: 2 + i for i in range(8)}
    flops = 2 * n_parts * tiles * tile * width * (4 * hidden + 768)
    scratch = [pltpu.VMEM((tile, width), BF), pltpu.VMEM((tile, width), BF)]
    if last:
        scratch.append(pltpu.VMEM((2 * width, hidden), F32))
    return pl.pallas_call(
        functools.partial(rows_kernel, n_parts, tiles, carried is not None, last),
        grid_spec=pltpu.PrefetchScalarGridSpec(
            num_scalar_prefetch=1,
            grid=(n_parts * tiles,),
            in_specs=in_specs,
            out_specs=out_specs,
            scratch_shapes=scratch,
        ),
        out_shape=out_shape,
        input_output_aliases=aliases,
        compiler_params=pltpu.CompilerParams(vmem_limit_bytes=52 * 2**20),
        cost_estimate=pl.CostEstimate(
            flops=flops // 8, bytes_accessed=2**20, transcendentals=0
        ),
        name="rows",
    )(place, *args)


def attention_kernel(block, first, final, waits, *refs):
    qq, dd, xh, ob, cosine, low, high, kk, vv = refs[:9]
    refs = refs[9:]
    if final:
        w_q, w_s, vecs = refs[:3]
        refs = refs[3:]
    refs = refs[waits:]
    if not first:
        k_in, v_in = refs[:2]
        ins = refs[2:7]
        refs = refs[7 + 3 :]
    if not final:
        k_out, v_out = refs[:2]
        refs = refs[2:]
    outs = refs[:5]
    g_q, g_out, g_s, b_q, b_s = outs
    context_out, query_out, shared_out = refs[5:8]
    refs = refs[8:]
    if final:
        payload, shared_sum, vectors = refs[:3]
        refs = refs[3:]
    s_scr, d_scr, k_sum, v_sum, o_acc, q_acc = refs
    heads = 3
    rows = heads * BLOCK
    n_tiles = block + 1

    for i, out in enumerate(outs):
        out[...] = jnp.zeros_like(out) if first else ins[i][...]

    left = lax.broadcasted_iota(jnp.int32, (BLOCK, LANES), 1) < HEAD_DIM
    zero = jnp.zeros((BLOCK, LANES), BF)

    def stack(ref):
        pair, last = ref[:, :LANES], ref[:, LANES:]
        return jnp.concatenate([jnp.where(left, pair, zero), jnp.where(left, zero, pair), last], 0)

    queries = stack(qq) * jnp.asarray(HEAD_DIM**-0.5, BF)
    incoming = stack(dd)
    queries_t = queries.T
    incoming_t = incoming.T

    def lanes(s, op):
        out = s[:, :LANES]
        for j in range(1, BLOCK // LANES):
            out = op(out, s[:, j * LANES : (j + 1) * LANES])
        return out

    peak = None
    for t in range(n_tiles):
        at = pl.ds(t * BLOCK, BLOCK)
        s = mm_cols(queries, kk[at, :])
        if t == block:
            key = lax.broadcasted_iota(jnp.int32, (BLOCK, BLOCK), 1)
            place = lax.broadcasted_iota(jnp.int32, (BLOCK, BLOCK), 0)
            s = jnp.where(jnp.concatenate([key <= place] * heads, 0), s, NEGATIVE)
        s_scr[:, at] = s
        top = lanes(s, jnp.maximum)
        peak = top if peak is None else jnp.maximum(peak, top)
    peak = jnp.max(peak, axis=1, keepdims=True)

    total = centre = jnp.zeros((rows, LANES), F32)
    for t in range(n_tiles):
        at = pl.ds(t * BLOCK, BLOCK)
        p = jnp.exp(s_scr[:, at] - peak)
        d = mm_cols(incoming, vv[at, :])
        s_scr[:, at] = p
        d_scr[:, at] = d
        part = mm(p.astype(BF), vv[at, :])
        if t == 0:
            o_acc[...] = part
        else:
            o_acc[...] += part
        total = total + lanes(p, jnp.add)
        centre = centre + lanes(p * d, jnp.add)
    inverse = 1.0 / jnp.sum(total, axis=1, keepdims=True)
    centre = jnp.sum(centre, axis=1, keepdims=True) * inverse

    for t in range(n_tiles):
        at = pl.ds(t * BLOCK, BLOCK)
        p = s_scr[:, at] * inverse
        ds = (p * (d_scr[:, at] - centre)).astype(BF)
        v_part = mm(incoming_t, p.astype(BF))
        k_part = mm(queries_t, ds)
        if not first:
            v_part = v_part + v_in[:, at]
            k_part = k_part + k_in[:, at]
        if t == block:
            v_sum[...] = v_part
            k_sum[...] = k_part
        else:
            v_out[:, at] = v_part
            k_out[:, at] = k_part
        part = mm(ds, kk[at, :])
        if t == 0:
            q_acc[...] = part
        else:
            q_acc[...] += part

    def unstack(a):
        return jnp.where(left, a[:BLOCK], a[BLOCK : 2 * BLOCK]), jnp.where(
            left, a[2 * BLOCK :], 0.0
        )

    c, l, h = cosine[...], low[...], high[...]
    mixed = o_acc[...] * inverse
    context = jnp.concatenate([a.astype(BF) for a in unstack(mixed)], 1)
    context_out[...] = context
    g_out[...] += mm_rows(ob[...], context)

    turned = unstack(q_acc[...] * HEAD_DIM**-0.5)
    query_back = jnp.concatenate([turn(a, c, l, h, -1.0).astype(BF) for a in turned], 1)
    key_back = k_sum[...].T
    value_back = v_sum[...].T
    key_back = turn(key_back + pltpu.roll(key_back, HEAD_DIM, 1), c, l, h, -1.0)
    value_back = value_back + pltpu.roll(value_back, HEAD_DIM, 1)
    shared_back = jnp.where(left, key_back, value_back).astype(BF)
    xhat = xh[...]
    g_q[...] += mm_rows(xhat, query_back)
    g_s[...] += mm_rows(xhat, shared_back)
    b_q[0:1, :] += jnp.sum(query_back.astype(F32), axis=0, keepdims=True)
    b_s[0:1, :] += jnp.sum(shared_back.astype(F32), axis=0, keepdims=True)
    query_out[...] = query_back
    shared_out[...] = shared_back

    if final:
        wq, ws = w_q[...].astype(F32), w_s[...].astype(F32)
        gq, go, gs = g_q[...], g_out[...], g_s[...]
        gain_back = jnp.sum(wq * gq, 1, keepdims=True) + jnp.sum(ws * gs, 1, keepdims=True)
        shift_back = jnp.sum(wq * b_q[0:1, :], 1, keepdims=True) + jnp.sum(
            ws * b_s[0:1, :], 1, keepdims=True
        )
        width = gq.shape[0]
        payload[:, :LANES] = gq[:, :LANES].astype(BF)
        payload[:, LANES : 2 * LANES] = go[:, :LANES].astype(BF)
        both = jnp.where(
            lax.broadcasted_iota(jnp.int32, (width, LANES), 1) < HEAD_DIM,
            gq[:, LANES:],
            pltpu.roll(go[:, LANES:], HEAD_DIM, 1),
        )
        payload[:, 2 * LANES :] = both.astype(BF)
        third = SMALL // 3
        for quarter in range(width // third // 3):
            for i in range(3):
                source = (3 * quarter + i) * third
                shared_sum[
                    quarter * third : (quarter + 1) * third, i * LANES : (i + 1) * LANES
                ] = gs[source : source + third, :].astype(BF)
        zeros = jnp.zeros((1, width), F32)
        s_row = jnp.concatenate([b_s[0:1, :], zeros[:, LANES:]], 1)
        q_row = jnp.concatenate([b_q[0:1, :], zeros[:, 2 * LANES :]], 1)
        listing = jnp.concatenate(
            [as_rows(gain_back, shift_back), vecs[0:2, :], s_row, vecs[2:4, :], q_row], 0
        )
        vectors[...] = jnp.concatenate([listing[:, : width // 2], listing[:, width // 2 :]], 0)


def attention_call(block, made, vecs, fixed, final, waits=(), carried=None):
    qq, kk, vv, dd, xh, ob = made
    group_rows, width = xh.shape
    first = carried is None
    seen = (block + 1) * BLOCK

    def placed(columns):
        return pl.BlockSpec((BLOCK, columns), lambda i: (block, 0))

    def whole(shape):
        return pl.BlockSpec(shape, lambda i: (0,) * len(shape))

    args = [qq, dd, xh, ob, *fixed["tables"]]
    in_specs = [placed(a.shape[1]) for a in args] + [whole((seen, LANES))] * 2
    args += [kk, vv]
    if final:
        full = [fixed["w_q"], fixed["w_s"], vecs]
        in_specs += [whole(a.shape) for a in full]
        args += full
    in_specs += [pl.BlockSpec(memory_space=pl.ANY)] * len(waits)
    args += list(waits)
    sums = [
        (width, 2 * LANES),
        (width, 2 * LANES),
        (width, LANES),
        (8, 2 * LANES),
        (8, LANES),
    ]
    shapes = ([] if final else [(LANES, block * BLOCK)] * 2) + sums
    out_shape = [jax.ShapeDtypeStruct(s, F32) for s in shapes]
    out_specs = [whole(s) for s in shapes]
    aliases = {}
    columns = [2 * LANES, 2 * LANES, LANES]
    if not first:
        start, at = len(args) + 7, len(shapes)
        in_specs += [whole(s) for s in [(LANES, seen)] * 2 + sums]
        in_specs += [pl.BlockSpec(memory_space=pl.ANY)] * 3
        args += list(carried)
        aliases = {start + i: at + i for i in range(3)}
    out_shape += [jax.ShapeDtypeStruct((group_rows, c), BF) for c in columns]
    out_specs += [placed(c) for c in columns]
    if final:
        last = [((width, 3 * LANES), BF), ((width // 3, 3 * LANES), BF), ((16, width // 2), F32)]
        out_shape += [jax.ShapeDtypeStruct(s, t) for s, t in last]
        out_specs += [whole(s) for s, _ in last]
    rows = 3 * BLOCK
    return pl.pallas_call(
        functools.partial(attention_kernel, block, first, final, len(waits)),
        grid=(1,),
        in_specs=in_specs,
        out_specs=out_specs,
        scratch_shapes=[
            pltpu.VMEM((rows, seen), F32),
            pltpu.VMEM((rows, seen), F32),
            pltpu.VMEM((LANES, BLOCK), F32),
            pltpu.VMEM((LANES, BLOCK), F32),
            pltpu.VMEM((rows, LANES), F32),
            pltpu.VMEM((rows, LANES), F32),
        ],
        out_shape=out_shape,
        input_output_aliases=aliases,
        compiler_params=pltpu.CompilerParams(vmem_limit_bytes=52 * 2**20),
        cost_estimate=pl.CostEstimate(
            flops=(block + 2) * 4 * 10**9, bytes_accessed=2**20, transcendentals=0
        ),
        name=f"attend{block}",
    )(*args)


def back_kernel(added, waits, place, *refs):
    act, back, context, query_back, shared_back = refs[:5]
    w_down, w_up, w_out, w_q, w_s, vec = refs[5:11]
    refs = refs[11:]
    branch = mm_cols(act[...], w_down[...]) + mm_cols(context[...], w_out[...])
    e = mm_cols(query_back[...], w_q[...]) + mm_cols(shared_back[...], w_s[...])
    w = e * vec[0:1, :] + mm_cols(back[...], w_up[...]) * vec[2:3, :]
    if added:
        branch = branch + refs[0][...].astype(F32)
        w = w + refs[1][...].astype(F32)
        refs = refs[2:]
    branch_out, w_out_ref = refs[waits:]
    branch_out[...] = branch.astype(branch_out.dtype)
    w_out_ref[...] = w.astype(w_out_ref.dtype)


def back_call(place, kept, fixed, own_rows, dtype, came=(), waits=()):
    width = kept[0].shape[1]

    def whole(a):
        return pl.BlockSpec(a.shape, lambda i, place: (0,) * a.ndim)

    full = [fixed[k] for k in ("w_down", "w_up", "w_out", "w_q", "w_s", "vec")] + list(came)
    in_specs = [
        pl.BlockSpec((own_rows, a.shape[1]), lambda i, place: (place[0], 0)) for a in kept
    ]
    in_specs += [whole(a) for a in full] + [pl.BlockSpec(memory_space=pl.ANY)] * len(waits)
    out = jax.ShapeDtypeStruct((own_rows, width), dtype)
    return pl.pallas_call(
        functools.partial(back_kernel, len(came) > 0, len(waits)),
        grid_spec=pltpu.PrefetchScalarGridSpec(
            num_scalar_prefetch=1,
            grid=(1,),
            in_specs=in_specs,
            out_specs=[pl.BlockSpec((own_rows, width), lambda i, place: (0, 0))] * 2,
        ),
        out_shape=[out, out],
        compiler_params=pltpu.CompilerParams(vmem_limit_bytes=32 * 2**20),
        cost_estimate=pl.CostEstimate(
            flops=10**7, bytes_accessed=2**14, transcendentals=0
        ),
        name="back",
    )(place, *kept, *full, *waits)


def swap(a, axis, bit):
    size = lax.axis_size(axis)
    return lax.ppermute(a, axis, [(i, i ^ bit) for i in range(size)])


def bits_of(size):
    return [1 << i for i in range(size.bit_length() - 1)]


def halving(a, axis, order):
    size = lax.axis_size(axis)
    index = lax.axis_index(axis)
    for bit in order:
        half = a.shape[0] // 2
        mine = (index // bit) % 2
        keep = lax.dynamic_slice_in_dim(a, mine * half, half, 0)
        send = lax.dynamic_slice_in_dim(a, (1 - mine) * half, half, 0)
        other = yield swap(send.astype(BF), axis, bit)
        a = keep.astype(F32) + other.astype(F32)
    return a


def doubling(a, axis, order):
    index = lax.axis_index(axis)
    a = a.astype(BF)
    for bit in order[::-1]:
        mine = (index // bit) % 2
        other = yield swap(a, axis, bit)
        first, second = jnp.where(mine == 0, a, other), jnp.where(mine == 0, other, a)
        a = jnp.concatenate([first, second], 0)
    return a


def summing(a, axis, order):
    a = yield from halving(a, axis, order)
    return (yield from doubling(a, axis, order))


class Chain:
    def __init__(self, steps):
        self.steps = steps
        self.waiting = next(steps)
        self.result = None

    def advance(self):
        try:
            self.waiting = self.steps.send(self.waiting)
        except StopIteration as stop:
            self.waiting, self.result = None, stop.value

    def finish(self):
        while self.waiting is not None:
            self.advance()
        return self.result


def together(chains, arrays=()):
    waiting, arrays = lax.optimization_barrier(([c.waiting for c in chains], list(arrays)))
    for chain, value in zip(chains, waiting):
        chain.waiting = value
    return arrays


def advance(chains):
    for chain in chains:
        if chain.waiting is not None:
            chain.advance()


def on_device(
    tokens,
    source_subset,
    subset_weight,
    output_cotangent,
    attention_gain,
    attention_shift,
    feed_gain,
    feed_shift,
    query_weight,
    query_bias,
    shared_weight,
    shared_bias,
    out_weight,
    up_weight,
    up_bias,
    down_weight,
    out_bias,
):
    own_rows, width = tokens.shape
    parts = lax.axis_size("tensor")
    group_rows = own_rows * parts
    me = lax.axis_index("tensor")
    per = own_rows // TILE
    n_blocks = group_rows // TILE

    half = own_rows // 2
    tok1 = swap(tokens, "tensor", 1)
    cot1 = swap(output_cotangent, "tensor", 1)
    tok2 = swap(tokens, "tensor", 2)
    cot2 = swap(output_cotangent, "tensor", 2)

    match = source_subset[0] == jnp.arange(subset_weight.shape[0], dtype=jnp.int32)
    scale = jnp.sum(jnp.where(match, subset_weight, 0.0))

    def pad(a, columns):
        return jnp.pad(a, ((0, 0), (0, columns - a.shape[1])))

    local = query_weight.shape[1]
    key_part, value_part = shared_weight[:, :HEAD_DIM], shared_weight[:, HEAD_DIM:]
    w_q = pad(query_weight, 2 * LANES)
    w_qkv = jnp.concatenate([w_q, key_part, key_part, value_part, value_part], 1)
    key_bias, value_bias = shared_bias[:HEAD_DIM], shared_bias[HEAD_DIM:]
    qkv_bias = jnp.concatenate(
        [
            jnp.pad(query_bias, (0, 2 * LANES - local)),
            key_bias,
            key_bias,
            value_bias,
            value_bias,
        ]
    ).astype(F32)[None, :]
    w_out = pad(out_weight, 2 * LANES)
    zeros = jnp.zeros_like(attention_gain)
    vec = jnp.stack(
        [
            attention_gain,
            attention_shift,
            feed_gain,
            feed_shift,
            up_bias.astype(F32),
            zeros,
            zeros,
            zeros,
        ]
    )
    fixed = {
        "vec": vec,
        "qkv_bias": qkv_bias,
        "tables": rope_tables(),
        "w_qkv": w_qkv,
        "w_up": up_weight,
        "w_down": down_weight,
        "w_out": w_out,
        "w_q": w_q,
        "w_s": shared_weight,
        "gain": attention_gain[None, :],
    }

    scale_in = scale.reshape(1, 1)
    chunk = [(me ^ k).astype(jnp.int32) for k in range(parts)]
    made = rows_call(
        [tokens, tok1],
        [output_cotangent, cot1],
        own_rows,
        jnp.stack(chunk[:2]),
        scale_in,
        fixed,
        group_rows,
    )
    tok2, cot2, first_vecs = lax.optimization_barrier((tok2, cot2, made[1]))
    made = rows_call(
        [tok2, swap(tok2, "tensor", 1)],
        [cot2, swap(cot2, "tensor", 1)],
        own_rows,
        jnp.stack(chunk[2:]),
        scale_in,
        fixed,
        group_rows,
        [made[0], first_vecs, *made[2:]],
        True,
    )
    sums, vecs, act, back = made[:4]
    made = made[4:]

    bits = bits_of(lax.axis_size("batch"))
    turned_bits = bits[1:] + bits[:1]
    down_chain = Chain(summing(sums[:width], "batch", bits))
    up_chain = Chain(summing(sums[width:], "batch", turned_bits))
    carried, waits = None, ()
    for block in range(group_rows // BLOCK)[::-1]:
        final = block == 0
        carried = attention_call(block, made, vecs, fixed, final, waits, carried)
        waits = tuple(c.waiting for c in (down_chain, up_chain))
        if not final:
            advance((down_chain, up_chain))
    *kept, payload, shared_sum, vectors = carried[5:]
    kept = [act, back, *kept]

    main = Chain(halving(payload, "batch", bits[:1]))
    small_rows = shared_sum.shape[0] // parts
    sent = [
        jnp.concatenate(
            [lax.dynamic_slice_in_dim(shared_sum, c * small_rows, small_rows, 0), vectors.astype(BF)],
            0,
        )
        for c in chunk
    ]
    others = [swap(sent[k], "tensor", k) for k in range(1, parts)]
    waits = (down_chain.waiting, up_chain.waiting)
    send3 = back_call(chunk[3].reshape(1), kept, fixed, own_rows, BF, (), waits)
    advance((down_chain, up_chain))
    got3 = [swap(a, "tensor", 1) for a in send3]
    send1 = back_call(chunk[1].reshape(1), kept, fixed, own_rows, BF, (), (*others,))
    got1 = [swap(a, "tensor", 1) for a in send1]
    mine = jnp.concatenate([sent[0][:small_rows].astype(F32), vectors], 0)
    every = mine
    for other in others:
        every = every + other.astype(F32)
    row = jnp.arange(small_rows + 16, dtype=jnp.int32)[:, None] - small_rows
    every = jnp.where((row >= 0) & (row % 8 >= 5), mine, every)
    near_x = swap(every.astype(BF), "batch", bits[0])
    far = back_call(
        chunk[2].reshape(1), kept, fixed, own_rows, BF, got3, (main.waiting, near_x)
    )
    main.advance()
    every = every + near_x.astype(F32)
    pieces = lax.axis_size("batch") // 2
    room = -(-every.shape[0] // (16 * pieces)) * 16 * pieces
    columns = every.shape[1]
    joined = jnp.concatenate(
        [
            main.result.reshape(pieces, -1, columns),
            jnp.pad(every, ((0, room - every.shape[0]), (0, 0))).reshape(pieces, -1, columns),
        ],
        1,
    )
    per_piece = joined.shape[1]
    main = Chain(summing(joined.reshape(-1, columns), "batch", bits[1:]))
    near = back_call(chunk[0].reshape(1), kept, fixed, own_rows, F32, got1)
    parts_y = [a[i * half : (i + 1) * half] for a in (far[1], far[0]) for i in range(2)]
    came = []
    for step in range(2 * (len(bits) - 1)):
        crossing = [swap(parts_y[step], "tensor", 2)] if step < len(parts_y) else []
        if step == 0:
            came += together((main, down_chain), crossing)
            advance((main, down_chain))
        elif step == 3:
            w = near[1] + jnp.concatenate(came[:2], 0).astype(F32)
            xhat, inverse = normalize(tokens.astype(F32))
            tokens_back = output_cotangent.astype(F32) * scale + inverse * (
                w
                - jnp.mean(w, axis=-1, keepdims=True)
                - xhat * jnp.mean(w * xhat, axis=-1, keepdims=True)
            )
            tokens_back, *crossing = together((main,), [tokens_back.astype(BF), *crossing])
            came += crossing
            advance((main,))
        else:
            came += together((main,), crossing)
            advance((main,))
    joined, up_chain.waiting = lax.optimization_barrier((main.result, up_chain.waiting))
    joined = joined.reshape(pieces, per_piece, columns)
    half_rows = payload.shape[0] // 2 // pieces
    every = joined[:, half_rows:].reshape(-1, columns)
    last = Chain(doubling(joined[:, :half_rows].reshape(-1, columns), "batch", bits[:1]))
    shared_parts = [every[:small_rows]]
    shared_parts += [swap(every[:small_rows], "tensor", k) for k in range(1, parts)]
    advance((up_chain,))
    vectors = every[small_rows : small_rows + 16]
    branch = near[0] + jnp.concatenate(came[2:], 0).astype(F32)
    mixed = (tokens.astype(F32) + branch + out_bias.astype(F32)).astype(BF)

    vectors = vectors.astype(F32)
    vectors = jnp.concatenate([vectors[:8], vectors[8:]], 1)
    gain_back, shift_back, feed_gain_back, feed_shift_back, b_s, up_back, out_back, b_q = vectors
    b_s, b_q = b_s[: 2 * HEAD_DIM], b_q[:local]
    stacked = jnp.stack(shared_parts)
    ordered = jnp.stack([lax.dynamic_index_in_dim(stacked, me ^ j, 0, False) for j in range(parts)])
    g_s = jnp.swapaxes(ordered.reshape(parts, small_rows, 3, LANES), 1, 2).reshape(-1, LANES)
    shared_back = g_s.astype(F32) * attention_gain[:, None] + attention_shift[:, None] * b_s[None, :]
    payload = last.finish().astype(F32)
    down_sum, up_sum = down_chain.finish(), up_chain.finish()
    g_q = jnp.concatenate([payload[:, :LANES], payload[:, 2 * LANES : 2 * LANES + HEAD_DIM]], 1)
    g_out = jnp.concatenate([payload[:, LANES : 2 * LANES], payload[:, 2 * LANES + HEAD_DIM :]], 1)
    query_back = g_q * attention_gain[:, None] + attention_shift[:, None] * b_q[None, :]
    up_back_matrix = up_sum.astype(F32) * feed_gain[:, None] + feed_shift[:, None] * up_back[None, :]
    return (
        mixed,
        tokens_back,
        gain_back,
        shift_back,
        feed_gain_back,
        feed_shift_back,
        query_back,
        b_q,
        shared_back,
        b_s,
        g_out,
        up_back_matrix,
        up_back,
        down_sum.astype(F32),
        out_back,
    )


def solution(mesh):
    return jax.shard_map(
        on_device,
        mesh=mesh,
        in_specs=(
            P(("batch", "tensor"), None),
            P("batch"),
            P(),
            P(("batch", "tensor"), None),
            P(),
            P(),
            P(),
            P(),
            P(None, "tensor"),
            P("tensor"),
            P(),
            P(),
            P(None, "tensor"),
            P(None, "tensor"),
            P("tensor"),
            P(None, "tensor"),
            P(),
        ),
        out_specs=(
            P(("batch", "tensor"), None),
            P(("batch", "tensor"), None),
            P(),
            P(),
            P(),
            P(),
            P(None, "tensor"),
            P("tensor"),
            P(),
            P(),
            P(None, "tensor"),
            P(None, "tensor"),
            P("tensor"),
            P(None, "tensor"),
            P(),
        ),
        check_vma=False,
    )
```

```python
import functools

import jax
import jax.numpy as jnp
import numpy as np
from jax import lax
from jax.experimental import pallas as pl
from jax.experimental.pallas import tpu as pltpu
from jax.sharding import PartitionSpec as P

HEAD_DIM = 64
LEN = 2048
ROT = 16
HALF = ROT // 2
BLOCK = 512
LANES = 128
SMALL = 192

EPSILON = 1e-05
NEGATIVE = -1e30
BF = jnp.bfloat16
F32 = jnp.float32


def near(a):
    return pltpu.with_memory_space_constraint(a, pltpu.VMEM)


def main_memory(a):
    return pltpu.with_memory_space_constraint(a, pltpu.HBM)


def mm(left, right):
    return jnp.dot(left, right, preferred_element_type=F32)


def mm_rows(left, right):
    return lax.dot_general(left, right, (((0,), (0,)), ((), ())), preferred_element_type=F32)


def mm_cols(left, right):
    return lax.dot_general(left, right, (((1,), (1,)), ((), ())), preferred_element_type=F32)


def rope_tables():
    lane = np.arange(LANES) % HEAD_DIM
    frequency = (10000.0 ** (-2.0 * np.arange(HALF, dtype=np.float32) / ROT)).astype(np.float32)
    angles = np.arange(LEN, dtype=np.float32)[:, None] * frequency[lane % HALF][None, :]
    angles = angles.astype(np.float32).astype(np.float64)
    turned = lane < ROT
    cosine = np.where(turned, np.cos(angles), 1.0)
    sine = np.where(lane < HALF, -np.sin(angles), np.where(turned, np.sin(angles), 0.0))
    return [jnp.asarray(t.astype(np.float32)) for t in (cosine, sine)]


def turn(values, cosine, sine, sign):
    lane = lax.broadcasted_iota(jnp.int32, values.shape, 1)
    up = pltpu.roll(values, LANES - HALF, 1)
    down = pltpu.roll(values, HALF, 1)
    return values * cosine + sign * sine * jnp.where(lane % HEAD_DIM < HALF, up, down)


def normalize(rows):
    centred = rows - jnp.mean(rows, axis=-1, keepdims=True)
    variance = jnp.mean(centred * centred, axis=-1, keepdims=True)
    scale = lax.rsqrt(variance + EPSILON)
    return centred * scale, scale


def pick(refs, n, scratch):
    pieces = len(refs) // n
    rows = refs[0].shape[0]
    for part in range(n):

        @pl.when(pl.program_id(0) == part)
        def _(part=part):
            for i in range(pieces):
                scratch[i * rows : (i + 1) * rows, :] = refs[part * pieces + i][...]

    return scratch[...]


def forward_part(x, vec, q_bias, s_bias, tables, w_q, w_s, w_up, xh, act, qq, kk, vv):
    xhat, _ = normalize(x.astype(F32))
    xhat_low = xhat.astype(BF)
    xh[...] = xhat_low
    attention_in = (xhat * vec[0:1, :] + vec[1:2, :]).astype(BF)
    feed_in = (xhat * vec[2:3, :] + vec[3:4, :]).astype(BF)
    hidden = mm(feed_in, w_up[...]) + vec[4:5, :]
    raw = mm(attention_in, w_q[...]) + q_bias[...]
    shared = mm(attention_in, w_s[...]) + s_bias[...]
    cdf = 0.5 + 0.5 * lax.erf(hidden * (0.5**0.5))
    slope = cdf + hidden * (jnp.exp(-0.5 * hidden * hidden) * (2.0 * np.pi) ** -0.5)
    activated = (hidden * cdf).astype(BF)
    act[...] = activated
    c, s = (t[...] for t in tables)
    qq[:, :LANES] = turn(raw[:, :LANES], c, s, 1.0).astype(BF)
    qq[:, LANES:] = turn(raw[:, LANES : 2 * LANES], c, s, 1.0).astype(BF)
    left = lax.broadcasted_iota(jnp.int32, shared.shape, 1) < HEAD_DIM
    twin = pltpu.roll(shared, HEAD_DIM, 1)
    kk[...] = turn(jnp.where(left, shared, twin), c, s, 1.0).astype(BF)
    vv[...] = jnp.where(left, twin, shared).astype(BF)
    return xhat_low, activated, slope


def backward_part(g, scale, xhat_low, activated, slope, w_down, w_out, sums, vecs, back, dd, ob):
    width = g.shape[1]
    outer = g.astype(F32) * scale[0, 0]
    outer_low = outer.astype(BF)
    ob[...] = outer_low
    vecs[3:4, :] += jnp.sum(outer, axis=0, keepdims=True)
    hidden_back = (mm(outer_low, w_down[...]) * slope).astype(BF)
    back[...] = hidden_back
    dd[...] = mm(outer_low, w_out[...]).astype(BF)
    sums[:width, :] += mm_rows(outer_low, activated)
    sums[width:, :] += mm_rows(xhat_low, hidden_back)
    vecs[2:3, :] += jnp.sum(hidden_back.astype(F32), axis=0, keepdims=True)


def first_kernel(n, place, scale, *refs):
    tokens, cots, refs = refs[:n], refs[n : 2 * n], refs[2 * n :]
    vec, q_bias, s_bias, *tables, w_q, w_s, w_up, w_down, w_out = refs[:10]
    sums, vecs, xh, act, qq, kk, vv, back, dd, ob, x_scr, g_scr = refs[10:]
    given = (vec, q_bias, s_bias, tables, w_q, w_s, w_up)

    @pl.when(pl.program_id(0) == 0)
    def _():
        sums[...] = jnp.zeros_like(sums)
        vecs[...] = jnp.zeros_like(vecs)

    x, g = pick(tokens, n, x_scr), pick(cots, n, g_scr)
    made = forward_part(x, *given, xh, act, qq, kk, vv)
    backward_part(g, scale, *made, w_down, w_out, sums, vecs, back, dd, ob)


def forward_kernel(n, pieces, place, *refs):
    tokens, refs = refs[: n * pieces], refs[n * pieces :]
    vec, q_bias, s_bias, *tables, w_q, w_s, w_up = refs[:8]
    xh, act, qq, kk, vv, slope, x_scr = refs[8 + 5 :]
    given = (vec, q_bias, s_bias, tables, w_q, w_s, w_up)
    x = pick(tokens, n, x_scr)
    *_, made = forward_part(x, *given, xh, act, qq, kk, vv)
    slope[...] = made.astype(BF)


def backward_kernel(n, pieces, place, scale, *refs):
    cots, refs = refs[: n * pieces], refs[n * pieces :]
    xh, act, slope, w_up, w_down, w_out, vecs_in, sums_in = refs[:8]
    sums_out, vecs, back, dd, ob, g_scr, sums = refs[8 + 3 :]
    step = pl.program_id(0)

    @pl.when(step == 0)
    def _():
        sums[...] = sums_in[...]
        vecs[...] = vecs_in[...]

    backward_part(
        pick(cots, n, g_scr),
        scale,
        xh[...],
        act[...],
        slope[...].astype(F32),
        w_down,
        w_out,
        sums,
        vecs,
        back,
        dd,
        ob,
    )

    @pl.when(step == pl.num_programs(0) - 1)
    def _():
        width = w_up.shape[0]
        sums_out[...] = sums[...].astype(BF)
        up_sum = sums[width:, :]
        up = w_up[...].astype(F32)
        gain_back = jnp.sum(up * up_sum, 1, keepdims=True)
        shift_back = jnp.sum(up * vecs[2:3, :], 1, keepdims=True)
        vecs[0:2, :] = as_rows(gain_back, shift_back)


def as_rows(first, second):
    lane = lax.broadcasted_iota(jnp.int32, (first.shape[0], LANES), 1)
    return jnp.where(lane == 0, first, second).T[:2, :]


def rows_call(kind, place, fixed, group_rows, scale=None, tokens=(), cots=(), carried=None, slope=None):
    n = place.shape[0]
    given = [*tokens, *cots]
    width = given[0].shape[1]
    rows = group_rows // fixed["parts"]
    hidden = fixed["w_up"].shape[1]
    anywhere = pl.BlockSpec(memory_space=pl.ANY)
    widths = {
        "xh": width,
        "act": hidden,
        "qq": 2 * LANES,
        "kk": LANES,
        "vv": LANES,
        "back": hidden,
        "dd": 2 * LANES,
        "ob": width,
    }
    sums_shape = (2 * width, hidden)

    def whole(shape):
        return pl.BlockSpec(shape, lambda i, place: (0,) * len(shape))

    def placed(columns):
        return pl.BlockSpec((rows, columns), lambda i, place: (place[i], 0))

    def in_turn(columns):
        return pl.BlockSpec((rows, columns), lambda i, place: (i, 0))

    args, in_specs = [], []
    kept_near = ("xh", "qq", "kk", "vv", "dd", "ob", "sums", "slope", "act", "back")

    def where(name):
        return near if name in kept_near else main_memory

    def take(arrays, specs):
        args.extend(arrays)
        in_specs.extend(specs)

    def full(*names):
        arrays = [near(fixed[k]) if k in ("w_up", "w_down") else fixed[k] for k in names]
        take(arrays, [whole(a.shape) for a in arrays])

    if scale is not None:
        take([scale], [pl.BlockSpec(memory_space=pltpu.SMEM)])
    take(given, [whole(a.shape) for a in given])
    outs, scratch = {}, []
    if kind == "backward":
        take([near(carried["xh"]), near(carried["act"])], [placed(width), placed(hidden)])
        take([near(slope)], [in_turn(hidden)])
        full("w_up", "w_down", "w_out")
        take([carried["vecs"], near(carried["sums"])], [whole((8, width)), whole(sums_shape)])
        names = ["back", "dd", "ob"]
        outs["sums"] = (sums_shape, BF, whole(sums_shape))
        outs["vecs"] = ((8, width), F32, whole((8, width)))
        scratch = [pltpu.VMEM((rows, width), BF)]
        scratch += [pltpu.VMEM(sums_shape, F32)]
    else:
        full("vec", "q_bias", "s_bias")
        take([near(t) for t in fixed["tables"]], [placed(LANES)] * 2)
        full("w_q", "w_s", "w_up")
        names = ["xh", "act", "qq", "kk", "vv"]
        scratch = [pltpu.VMEM((rows, width), BF)]
        if kind == "first":
            full("w_down", "w_out")
            names += ["back", "dd", "ob"]
            outs["sums"] = (sums_shape, F32, whole(sums_shape))
            outs["vecs"] = ((8, width), F32, whole((8, width)))
            scratch = scratch * 2
    aliases = {}
    for k in names:
        if carried is not None:
            aliases[len(args) + 1] = len(outs)
            take([where(k)(carried[k])], [anywhere])
        outs[k] = ((group_rows, widths[k]), BF, placed(widths[k]))
    if kind == "forward":
        outs["slope"] = ((n * rows, hidden), BF, in_turn(hidden))
    kernel = {
        "first": functools.partial(first_kernel, n),
        "forward": functools.partial(forward_kernel, n, len(tokens) // n),
        "backward": functools.partial(backward_kernel, n, len(cots) // n),
    }[kind]
    results = pl.pallas_call(
        kernel,
        grid_spec=pltpu.PrefetchScalarGridSpec(
            num_scalar_prefetch=1,
            grid=(n,),
            in_specs=in_specs,
            out_specs=[spec for *_, spec in outs.values()],
            scratch_shapes=scratch,
        ),
        out_shape=[
            (pltpu.VMEM if k in kept_near else pltpu.HBM)(shape, kind_)
            for k, (shape, kind_, _) in outs.items()
        ],
        input_output_aliases=aliases,
        compiler_params=pltpu.CompilerParams(vmem_limit_bytes=13 * 2**20),
        cost_estimate=pl.CostEstimate(
            flops=n * 4 * 10**8, bytes_accessed=2**20, transcendentals=0
        ),
        name=f"rows_{kind}",
    )(place, *args)
    return {**(carried or {}), **dict(zip(outs, results))}


def attention_kernel(block, first, final, waits, *refs):
    qq, dd, kk, vv, cosine, sine, ob, xh = refs[:8]
    refs = refs[8:]
    if final:
        w_q, w_s, vecs = refs[:3]
        refs = refs[3:]
    refs = refs[waits:]
    if not first:
        carried = refs[:7]
        refs = refs[7 + 3 :]
    if not final:
        k_out, v_out, *sums_out = refs[:7]
        refs = refs[7:]
    context_out, query_out, shared_out = refs[:3]
    refs = refs[3:]
    if final:
        payload, shared_sum, vectors = refs[:3]
        refs = refs[3:]
    s_scr, d_scr, k_acc, v_acc = refs[:4]
    if final:
        sums_out = refs[4:]
    g_out, g_q, g_s, b_q, b_s = sums_out
    here = pl.ds(block * BLOCK, BLOCK)

    def add(which, value):
        sums_out[which][...] = value if first else carried[2 + which][...] + value

    def column_sum(a):
        return jnp.broadcast_to(jnp.sum(a.astype(F32), axis=0, keepdims=True), (8, a.shape[1]))

    left = lax.broadcasted_iota(jnp.int32, (BLOCK, LANES), 1) < HEAD_DIM
    zero = jnp.zeros((BLOCK, LANES), BF)

    def split(ref):
        pair, last = ref[:, :LANES], ref[:, LANES:]
        return jnp.where(left, pair, zero), jnp.where(left, zero, pair), last

    def lanes(s, op):
        out = s[:, :LANES]
        for j in range(1, BLOCK // LANES):
            out = op(out, s[:, j * LANES : (j + 1) * LANES])
        return out

    mixed, turned = [], []
    for head, (queries, incoming) in enumerate(zip(split(qq[here, :]), split(dd[here, :]))):
        queries = queries * jnp.asarray(HEAD_DIM**-0.5, BF)
        queries_t, incoming_t = queries.T, incoming.T
        slot = head % 2
        peak = None
        for t in range(block + 1):
            at = pl.ds(t * BLOCK, BLOCK)
            s = mm_cols(queries, kk[at, :])
            if t == block:
                key = lax.broadcasted_iota(jnp.int32, (BLOCK, BLOCK), 1)
                place = lax.broadcasted_iota(jnp.int32, (BLOCK, BLOCK), 0)
                s = jnp.where(key <= place, s, NEGATIVE)
            s_scr[slot, :, at] = s
            top = lanes(s, jnp.maximum)
            peak = top if peak is None else jnp.maximum(peak, top)
        peak = jnp.max(peak, axis=1, keepdims=True)

        total = centre = jnp.zeros((BLOCK, LANES), F32)
        out = None
        for t in range(block + 1):
            at = pl.ds(t * BLOCK, BLOCK)
            p = jnp.exp(s_scr[slot, :, at] - peak)
            d = mm_cols(incoming, vv[at, :])
            s_scr[slot, :, at] = p
            d_scr[slot, :, at] = d
            part = mm(p.astype(BF), vv[at, :])
            out = part if out is None else out + part
            total = total + lanes(p, jnp.add)
            centre = centre + lanes(p * d, jnp.add)
        inverse = 1.0 / jnp.sum(total, axis=1, keepdims=True)
        centre = jnp.sum(centre, axis=1, keepdims=True) * inverse
        mixed.append(out * inverse)

        out = None
        for t in range(block + 1):
            at = pl.ds(t * BLOCK, BLOCK)
            p = s_scr[slot, :, at] * inverse
            ds = (p * (d_scr[slot, :, at] - centre)).astype(BF)
            v_part = mm(incoming_t, p.astype(BF))
            k_part = mm(queries_t, ds)
            if head == 0 and first:
                v_acc[:, at] = v_part
                k_acc[:, at] = k_part
            elif head == 0:
                v_acc[:, at] = carried[1][:, at] + v_part
                k_acc[:, at] = carried[0][:, at] + k_part
            else:
                v_acc[:, at] += v_part
                k_acc[:, at] += k_part
            part = mm(ds, kk[at, :])
            out = part if out is None else out + part
        turned.append(out * HEAD_DIM**-0.5)
    if not final:
        k_out[...] = k_acc[:, : block * BLOCK]
        v_out[...] = v_acc[:, : block * BLOCK]

    def unstack(a):
        return jnp.where(left, a[0], a[1]), jnp.where(left, a[2], 0.0)

    c, s = cosine[here, :], sine[here, :]
    context = jnp.concatenate([a.astype(BF) for a in unstack(mixed)], 1)
    context_out[...] = context
    add(0, mm_rows(ob[here, :], context))

    query_back = jnp.concatenate(
        [turn(a, c, s, -1.0).astype(BF) for a in unstack(turned)], 1
    )
    key_back = k_acc[:, here].T
    value_back = v_acc[:, here].T
    key_back = turn(key_back + pltpu.roll(key_back, HEAD_DIM, 1), c, s, -1.0)
    value_back = value_back + pltpu.roll(value_back, HEAD_DIM, 1)
    shared_back = jnp.where(left, key_back, value_back).astype(BF)
    xhat = xh[here, :]
    add(1, mm_rows(xhat, query_back))
    add(2, mm_rows(xhat, shared_back))
    add(3, column_sum(query_back))
    add(4, column_sum(shared_back))
    query_out[...] = query_back
    shared_out[...] = shared_back

    if final:
        wq, ws = w_q[...].astype(F32), w_s[...].astype(F32)
        gq, go, gs = g_q[...], g_out[...], g_s[...]
        gain_back = jnp.sum(wq * gq, 1, keepdims=True) + jnp.sum(ws * gs, 1, keepdims=True)
        shift_back = jnp.sum(wq * b_q[0:1, :], 1, keepdims=True) + jnp.sum(
            ws * b_s[0:1, :], 1, keepdims=True
        )
        width = gq.shape[0]
        payload[:, :LANES] = gq[:, :LANES].astype(BF)
        payload[:, LANES : 2 * LANES] = go[:, :LANES].astype(BF)
        both = jnp.where(
            lax.broadcasted_iota(jnp.int32, (width, LANES), 1) < HEAD_DIM,
            gq[:, LANES:],
            pltpu.roll(go[:, LANES:], HEAD_DIM, 1),
        )
        payload[:, 2 * LANES :] = both.astype(BF)
        third = SMALL // 3
        for quarter in range(width // third // 3):
            for i in range(3):
                source = (3 * quarter + i) * third
                shared_sum[
                    quarter * third : (quarter + 1) * third, i * LANES : (i + 1) * LANES
                ] = gs[source : source + third, :].astype(BF)
        zeros = jnp.zeros((1, width), F32)
        s_row = jnp.concatenate([b_s[0:1, :], zeros[:, LANES:]], 1)
        q_row = jnp.concatenate([b_q[0:1, :], zeros[:, 2 * LANES :]], 1)
        listing = jnp.concatenate(
            [as_rows(gain_back, shift_back), vecs[0:2, :], s_row, vecs[2:4, :], q_row], 0
        )
        vectors[...] = jnp.concatenate([listing[:, : width // 2], listing[:, width // 2 :]], 0)


def attention_call(block, made, vecs, fixed, final, waits=(), carried=None):
    qq, kk, vv, dd, xh, ob = made
    group_rows, width = xh.shape
    first = carried is None
    seen = (block + 1) * BLOCK

    def placed(columns):
        return pl.BlockSpec((BLOCK, columns), lambda i: (block, 0))

    def whole(shape):
        return pl.BlockSpec(shape, lambda i: (0,) * len(shape))

    anywhere = pl.BlockSpec(memory_space=pl.ANY)
    args = [near(a) for a in (qq, dd, kk, vv, *fixed["tables"], ob, xh)]
    in_specs = [whole(a.shape) for a in args]
    if final:
        full = [fixed["w_q"], fixed["w_s"], vecs]
        in_specs += [whole(a.shape) for a in full]
        args += full
    in_specs += [anywhere] * len(waits)
    args += list(waits)
    sums = [
        (width, 2 * LANES),
        (width, 2 * LANES),
        (width, LANES),
        (8, 2 * LANES),
        (8, LANES),
    ]
    shapes = [] if final else [(LANES, block * BLOCK)] * 2 + sums
    out_shape = [pltpu.VMEM(s, F32) for s in shapes]
    out_specs = [whole(s) for s in shapes]
    aliases = {}
    columns = [2 * LANES, 2 * LANES, LANES]
    if not first:
        start, at = len(args) + 7, len(shapes)
        in_specs += [whole(a.shape) for a in carried[:7]] + [anywhere] * 3
        args += [near(a) for a in carried]
        aliases = {start + i: at + i for i in range(3)}
    out_shape += [pltpu.VMEM((group_rows, c), BF) for c in columns]
    out_specs += [placed(c) for c in columns]
    if final:
        last = [((width, 3 * LANES), BF), ((width // 3, 3 * LANES), BF), ((16, width // 2), F32)]
        out_shape += [jax.ShapeDtypeStruct(s, t) for s, t in last]
        out_specs += [whole(s) for s, _ in last]
    scratch = [
        pltpu.VMEM((2, BLOCK, seen), F32),
        pltpu.VMEM((2, BLOCK, seen), F32),
        pltpu.VMEM((LANES, seen), F32),
        pltpu.VMEM((LANES, seen), F32),
        *[pltpu.VMEM(s, F32) for s in (sums if final else [])],
    ]
    return pl.pallas_call(
        functools.partial(attention_kernel, block, first, final, len(waits)),
        grid=(1,),
        in_specs=in_specs,
        out_specs=out_specs,
        scratch_shapes=scratch,
        out_shape=out_shape,
        input_output_aliases=aliases,
        compiler_params=pltpu.CompilerParams(vmem_limit_bytes=(2 + 5 * (block + 1)) * 2**20),
        cost_estimate=pl.CostEstimate(
            flops=(block + 2) * 4 * 10**9, bytes_accessed=2**20, transcendentals=0
        ),
        name=f"attend{block}",
    )(*args)


def back_kernel(added, waits, place, *refs):
    act, back, context, query_back, shared_back = refs[:5]
    w_down, w_up, w_out, w_q, w_s, vec = refs[5:11]
    refs = refs[11:]
    branch = mm_cols(act[...], w_down[...]) + mm_cols(context[...], w_out[...])
    e = mm_cols(query_back[...], w_q[...]) + mm_cols(shared_back[...], w_s[...])
    w = e * vec[0:1, :] + mm_cols(back[...], w_up[...]) * vec[2:3, :]
    if added:
        branch = branch + refs[0][...].astype(F32)
        w = w + refs[1][...].astype(F32)
        refs = refs[2:]
    branch_out, w_out_ref = refs[waits:]
    branch_out[...] = branch.astype(branch_out.dtype)
    w_out_ref[...] = w.astype(w_out_ref.dtype)


def back_call(place, kept, fixed, own_rows, dtype, came=(), waits=()):
    width = kept[0].shape[1]

    def whole(a):
        return pl.BlockSpec(a.shape, lambda i, place: (0,) * a.ndim)

    full = [fixed[k] for k in ("w_down", "w_up", "w_out", "w_q", "w_s", "vec")] + list(came)
    in_specs = [
        pl.BlockSpec((own_rows, a.shape[1]), lambda i, place: (place[0], 0)) for a in kept
    ]
    in_specs += [whole(a) for a in full] + [pl.BlockSpec(memory_space=pl.ANY)] * len(waits)
    kept = [near(a) for a in kept]
    full = [near(a) for a in full[:2]] + full[2:]
    out = jax.ShapeDtypeStruct((own_rows, width), dtype)
    return pl.pallas_call(
        functools.partial(back_kernel, len(came) > 0, len(waits)),
        grid_spec=pltpu.PrefetchScalarGridSpec(
            num_scalar_prefetch=1,
            grid=(1,),
            in_specs=in_specs,
            out_specs=[pl.BlockSpec((own_rows, width), lambda i, place: (0, 0))] * 2,
        ),
        out_shape=[out, out],
        compiler_params=pltpu.CompilerParams(vmem_limit_bytes=10 * 2**20),
        cost_estimate=pl.CostEstimate(
            flops=8 * 10**9, bytes_accessed=2**20, transcendentals=0
        ),
        name="back",
    )(place, *kept, *full, *waits)


def swap(a, axis, bit):
    size = lax.axis_size(axis)
    return lax.ppermute(a, axis, [(i, i ^ bit) for i in range(size)])


def bits_of(size):
    return [1 << i for i in range(size.bit_length() - 1)]


def halving(a, axis, order):
    size = lax.axis_size(axis)
    index = lax.axis_index(axis)
    for bit in order:
        half = a.shape[0] // 2
        mine = (index // bit) % 2
        keep = lax.dynamic_slice_in_dim(a, mine * half, half, 0)
        send = lax.dynamic_slice_in_dim(a, (1 - mine) * half, half, 0)
        other = yield swap(send.astype(BF), axis, bit)
        a = keep.astype(F32) + other.astype(F32)
    return a


def doubling(a, axis, order):
    index = lax.axis_index(axis)
    a = a.astype(BF)
    for bit in order[::-1]:
        mine = (index // bit) % 2
        other = yield swap(a, axis, bit)
        first, second = jnp.where(mine == 0, a, other), jnp.where(mine == 0, other, a)
        a = jnp.concatenate([first, second], 0)
    return a


def summing(a, axis, order):
    a = yield from halving(a, axis, order)
    return (yield from doubling(a, axis, order))


class Chain:
    def __init__(self, steps):
        self.steps = steps
        self.waiting = next(steps)
        self.result = None

    def advance(self):
        try:
            self.waiting = self.steps.send(self.waiting)
        except StopIteration as stop:
            self.waiting, self.result = None, stop.value

    def finish(self):
        while self.waiting is not None:
            self.advance()
        return self.result


def together(chains, arrays=()):
    waiting, arrays = lax.optimization_barrier(([c.waiting for c in chains], list(arrays)))
    for chain, value in zip(chains, waiting):
        chain.waiting = value
    return arrays


def advance(chains):
    for chain in chains:
        if chain.waiting is not None:
            chain.advance()


def on_device(
    tokens,
    source_subset,
    subset_weight,
    output_cotangent,
    attention_gain,
    attention_shift,
    feed_gain,
    feed_shift,
    query_weight,
    query_bias,
    shared_weight,
    shared_bias,
    out_weight,
    up_weight,
    up_bias,
    down_weight,
    out_bias,
):
    own_rows, width = tokens.shape
    parts = lax.axis_size("tensor")
    group_rows = own_rows * parts
    me = lax.axis_index("tensor")

    half = own_rows // 2
    tok1 = swap(tokens, "tensor", 1)
    cot1 = swap(output_cotangent, "tensor", 1)
    tok2 = [swap(tokens[i * half : (i + 1) * half], "tensor", 2) for i in range(2)]
    cot2 = [swap(output_cotangent[i * half : (i + 1) * half], "tensor", 2) for i in range(2)]

    match = source_subset[0] == jnp.arange(subset_weight.shape[0], dtype=jnp.int32)
    scale = jnp.sum(jnp.where(match, subset_weight, 0.0))

    def pad(a, columns):
        return jnp.pad(a, ((0, 0), (0, columns - a.shape[1])))

    local = query_weight.shape[1]
    w_q = pad(query_weight, 2 * LANES)
    w_out = pad(out_weight, 2 * LANES)
    row = lax.broadcasted_iota(jnp.int32, (8, width), 0)
    vec = jnp.zeros((8, width), F32)
    listed = (attention_gain, attention_shift, feed_gain, feed_shift, up_bias.astype(F32))
    for i, entry in enumerate(listed):
        vec = jnp.where(row == i, entry[None, :], vec)
    fixed = {
        "vec": vec,
        "q_bias": pad(query_bias[None, :].astype(F32), 2 * LANES),
        "s_bias": shared_bias[None, :].astype(F32),
        "tables": rope_tables(),
        "w_up": up_weight,
        "w_down": down_weight,
        "w_out": w_out,
        "w_q": w_q,
        "w_s": shared_weight,
        "parts": parts,
    }

    scale_in = scale.reshape(1, 1)
    chunk = [(me ^ k).astype(jnp.int32) for k in range(parts)]
    made = rows_call(
        "first",
        jnp.stack(chunk[:2]),
        fixed,
        group_rows,
        scale_in,
        [tokens, tok1],
        [output_cotangent, cot1],
    )
    far_places = jnp.stack(chunk[2:])
    *tok2, cot2[0], made["xh"] = lax.optimization_barrier((*tok2, cot2[0], made["xh"]))
    tok3 = [swap(a, "tensor", 1) for a in tok2]
    cot3 = [swap(cot2[0], "tensor", 1)]
    made = rows_call(
        "forward", far_places, fixed, group_rows, None, tok2 + tok3, (), made
    )
    cot2[1], slope = lax.optimization_barrier((cot2[1], made.pop("slope")))
    cot3.append(swap(cot2[1], "tensor", 1))
    made = rows_call(
        "backward", far_places, fixed, group_rows, scale_in, (), cot2 + cot3, made, slope
    )
    sums, vecs, act, back = (made[k] for k in ("sums", "vecs", "act", "back"))
    made = [made[k] for k in ("qq", "kk", "vv", "dd", "xh", "ob")]

    bits = bits_of(lax.axis_size("batch"))
    turned_bits = bits[1:] + bits[:1]
    down_chain = Chain(summing(sums[:width], "batch", bits))
    up_chain = Chain(summing(sums[width:], "batch", turned_bits))
    carried, waits = None, ()
    for block in range(group_rows // BLOCK)[::-1]:
        final = block == 0
        carried = attention_call(block, made, vecs, fixed, final, waits, carried)
        waits = tuple(c.waiting for c in (down_chain, up_chain))
        if not final:
            advance((down_chain, up_chain))
    *kept, payload, shared_sum, vectors = carried
    kept = [act, back, *kept]

    small_rows = shared_sum.shape[0] // parts
    sent = [
        jnp.concatenate(
            [lax.dynamic_slice_in_dim(shared_sum, c * small_rows, small_rows, 0), vectors.astype(BF)],
            0,
        )
        for c in chunk
    ]
    others = [swap(sent[k], "tensor", k) for k in range(1, parts)]
    send3 = back_call(chunk[3].reshape(1), kept, fixed, own_rows, BF)
    got3 = [swap(a, "tensor", 1) for a in send3]
    send1 = back_call(chunk[1].reshape(1), kept, fixed, own_rows, BF, (), (*others,))
    got1 = [swap(a, "tensor", 1) for a in send1]
    own = jnp.concatenate([sent[0][:small_rows].astype(F32), vectors], 0)
    every = own
    for other in others:
        every = every + other.astype(F32)
    row = jnp.arange(small_rows + 16, dtype=jnp.int32)[:, None] - small_rows
    every = jnp.where((row >= 0) & (row % 8 >= 5), own, every)
    pieces = lax.axis_size("batch")
    columns = payload.shape[1]
    room = -(-every.shape[0] // (16 * pieces)) * 16 * pieces
    every = jnp.pad(every.astype(BF), ((0, room - every.shape[0]), (0, 0)))
    joined = jnp.concatenate(
        [payload.reshape(pieces, -1, columns), every.reshape(pieces, -1, columns)], 1
    )
    per_piece, main_rows = joined.shape[1], payload.shape[0] // pieces
    main = Chain(summing(joined.reshape(-1, columns), "batch", bits))
    gradients = (down_chain, up_chain)
    far = back_call(chunk[2].reshape(1), kept, fixed, own_rows, BF, got3)
    near = back_call(chunk[0].reshape(1), kept, fixed, own_rows, F32, got1)
    parts_y = [a[i * half : (i + 1) * half] for a in (far[1], far[0]) for i in range(2)]
    came = []
    w = near[1]
    for step in range(2 * len(bits) - 1):
        crossing = [swap(parts_y[step - 1], "tensor", 2)] if 0 < step <= len(parts_y) else []
        now = {0: (main, *gradients), 1: (main, down_chain), 3: (main, up_chain)}.get(step, (main,))
        if step == 4:
            w = near[1] + jnp.concatenate(came[:2], 0).astype(F32)
            xhat, inverse = normalize(tokens.astype(F32))
            tokens_back = output_cotangent.astype(F32) * scale + inverse * (
                w
                - jnp.mean(w, axis=-1, keepdims=True)
                - xhat * jnp.mean(w * xhat, axis=-1, keepdims=True)
            )
            tokens_back, *crossing = together(now, [tokens_back.astype(BF), *crossing])
        else:
            crossing = together(now, crossing)
        came += crossing
        advance(now)
    main.advance()
    joined = main.result.reshape(pieces, per_piece, columns)
    every = joined[:, main_rows:].reshape(-1, columns)
    payload = joined[:, :main_rows].reshape(-1, columns).astype(F32)
    shared_parts = [every[:small_rows]]
    shared_parts += [swap(every[:small_rows], "tensor", k) for k in range(1, parts)]
    vectors = every[small_rows : small_rows + 16]
    branch = near[0] + jnp.concatenate(came[2:], 0).astype(F32)
    mixed = (tokens.astype(F32) + branch + out_bias.astype(F32)).astype(BF)

    vectors = vectors.astype(F32)
    vectors = jnp.concatenate([vectors[:8], vectors[8:]], 1)
    gain_back, shift_back, feed_gain_back, feed_shift_back, b_s, up_back, out_back, b_q = vectors
    b_s, b_q = b_s[: 2 * HEAD_DIM], b_q[:local]
    stacked = jnp.stack(shared_parts)
    ordered = jnp.stack([lax.dynamic_index_in_dim(stacked, me ^ j, 0, False) for j in range(parts)])
    g_s = jnp.swapaxes(ordered.reshape(parts, small_rows, 3, LANES), 1, 2).reshape(-1, LANES)
    shared_back = g_s.astype(F32) * attention_gain[:, None] + attention_shift[:, None] * b_s[None, :]
    down_sum, up_sum = down_chain.finish(), up_chain.finish()
    g_q = jnp.concatenate([payload[:, :LANES], payload[:, 2 * LANES : 2 * LANES + HEAD_DIM]], 1)
    g_out = jnp.concatenate([payload[:, LANES : 2 * LANES], payload[:, 2 * LANES + HEAD_DIM :]], 1)
    query_back = g_q * attention_gain[:, None] + attention_shift[:, None] * b_q[None, :]
    up_back_matrix = up_sum.astype(F32) * feed_gain[:, None] + feed_shift[:, None] * up_back[None, :]
    return (
        mixed,
        tokens_back,
        gain_back,
        shift_back,
        feed_gain_back,
        feed_shift_back,
        query_back,
        b_q,
        shared_back,
        b_s,
        g_out,
        up_back_matrix,
        up_back,
        down_sum.astype(F32),
        out_back,
    )


def solution(mesh):
    return jax.shard_map(
        on_device,
        mesh=mesh,
        in_specs=(
            P(("batch", "tensor"), None),
            P("batch"),
            P(),
            P(("batch", "tensor"), None),
            P(),
            P(),
            P(),
            P(),
            P(None, "tensor"),
            P("tensor"),
            P(),
            P(),
            P(None, "tensor"),
            P(None, "tensor"),
            P("tensor"),
            P(None, "tensor"),
            P(),
        ),
        out_specs=(
            P(("batch", "tensor"), None),
            P(("batch", "tensor"), None),
            P(),
            P(),
            P(),
            P(),
            P(None, "tensor"),
            P("tensor"),
            P(),
            P(),
            P(None, "tensor"),
            P(None, "tensor"),
            P("tensor"),
            P(None, "tensor"),
            P(),
        ),
        check_vma=False,
    )
```

```python
import functools

import jax
import jax.numpy as jnp
import numpy as np
from jax import lax
from jax.experimental import pallas as pl
from jax.experimental.pallas import tpu as pltpu
from jax.sharding import PartitionSpec as P

HEAD_DIM = 64
LEN = 2048
ROT = 16
HALF = ROT // 2
BLOCK = 512
LANES = 128
VECTORS = ("a_gain", "a_shift", "f_gain", "f_shift", "up_bias", "q_bias", "s_bias")

EPSILON = 1e-05
NEGATIVE = -1e30
BF = jnp.bfloat16
F32 = jnp.float32


def near(a):
    return pltpu.with_memory_space_constraint(a, pltpu.VMEM)


def main_memory(a):
    return pltpu.with_memory_space_constraint(a, pltpu.HBM)


def mm(left, right):
    return jnp.dot(left, right, preferred_element_type=F32)


def mm_rows(left, right):
    return lax.dot_general(left, right, (((0,), (0,)), ((), ())), preferred_element_type=F32)


def mm_cols(left, right):
    return lax.dot_general(left, right, (((1,), (1,)), ((), ())), preferred_element_type=F32)


def rope_tables():
    lane = np.arange(LANES) % HEAD_DIM
    frequency = (10000.0 ** (-2.0 * np.arange(HALF, dtype=np.float32) / ROT)).astype(np.float32)
    angles = np.arange(LEN, dtype=np.float32)[:, None] * frequency[lane % HALF][None, :]
    angles = angles.astype(np.float32).astype(np.float64)
    turned = lane < ROT
    cosine = np.where(turned, np.cos(angles), 1.0)
    sine = np.where(lane < HALF, -np.sin(angles), np.where(turned, np.sin(angles), 0.0))
    return [jnp.asarray(t.astype(np.float32)) for t in (cosine, sine)]


def turn(values, cosine, sine, sign):
    lane = lax.broadcasted_iota(jnp.int32, values.shape, 1)
    up = pltpu.roll(values, LANES - HALF, 1)
    down = pltpu.roll(values, HALF, 1)
    return values * cosine + sign * sine * jnp.where(lane % HEAD_DIM < HALF, up, down)


def normalize(rows):
    centred = rows - jnp.mean(rows, axis=-1, keepdims=True)
    variance = jnp.mean(centred * centred, axis=-1, keepdims=True)
    scale = lax.rsqrt(variance + EPSILON)
    return centred * scale, scale


def pick(refs, n, scratch):
    pieces = len(refs) // n
    rows = refs[0].shape[0]
    for part in range(n):

        @pl.when(pl.program_id(0) == part)
        def _(part=part):
            for i in range(pieces):
                scratch[i * rows : (i + 1) * rows, :] = refs[part * pieces + i][...]

    return scratch[...]


def two_slabs(a):
    rest = a[:, LANES:]
    filler = jnp.zeros((a.shape[0], 2 * LANES - a.shape[1]), a.dtype)
    return a[:, :LANES], jnp.concatenate([rest, filler], 1)


def line(ref):
    return ref[...].astype(F32)[None, :]


def forward_part(x, vectors, tables, w_q, w_s, w_up, xh, act, qq, kk, vv):
    xhat, _ = normalize(x.astype(F32))
    xhat_low = xhat.astype(BF)
    xh[...] = xhat_low
    a_gain, a_shift, f_gain, f_shift, up_bias, q_bias, s_bias = (line(v) for v in vectors)
    attention_in = (xhat * a_gain + a_shift).astype(BF)
    feed_in = (xhat * f_gain + f_shift).astype(BF)
    hidden = mm(feed_in, w_up[...]) + up_bias
    raw = mm_cols(attention_in, w_q[...]) + q_bias
    shared = mm(attention_in, w_s[...]) + s_bias
    cdf = 0.5 + 0.5 * lax.erf(hidden * (0.5**0.5))
    slope = cdf + hidden * (jnp.exp(-0.5 * hidden * hidden) * (2.0 * np.pi) ** -0.5)
    activated = (hidden * cdf).astype(BF)
    act[...] = activated
    c, s = (t[...] for t in tables)
    pair, last = two_slabs(raw)
    qq[:, :LANES] = turn(pair, c, s, 1.0).astype(BF)
    qq[:, LANES:] = turn(last, c, s, 1.0).astype(BF)
    left = lax.broadcasted_iota(jnp.int32, shared.shape, 1) < HEAD_DIM
    twin = pltpu.roll(shared, HEAD_DIM, 1)
    kk[...] = turn(jnp.where(left, shared, twin), c, s, 1.0).astype(BF)
    vv[...] = jnp.where(left, twin, shared).astype(BF)
    return xhat_low, activated, slope


def backward_part(g, scale, xhat_low, activated, slope, w_down, w_out, sums, vecs, back, dd, ob):
    width = g.shape[1]
    outer = g.astype(F32) * scale
    outer_low = outer.astype(BF)
    ob[...] = outer_low
    vecs[3:4, :] += jnp.sum(outer, axis=0, keepdims=True)
    hidden_back = (mm(outer_low, w_down[...]) * slope).astype(BF)
    back[...] = hidden_back
    pair, last = two_slabs(mm_cols(outer_low, w_out[...]))
    dd[:, :LANES] = pair.astype(BF)
    dd[:, LANES:] = last.astype(BF)
    sums[:width, :] += mm_rows(outer_low, activated)
    sums[width:, :] += mm_rows(xhat_low, hidden_back)
    vecs[2:3, :] += jnp.sum(hidden_back.astype(F32), axis=0, keepdims=True)


def first_kernel(n, place, subset, weight, *refs):
    scale = weight[subset[0]]
    tokens, cots, refs = refs[:n], refs[n : 2 * n], refs[2 * n :]
    *tables, w_q, w_s, w_up, w_down, w_out = refs[7:14]
    sums, vecs, xh, act, qq, kk, vv, back, dd, ob, x_scr, g_scr = refs[14:]
    given = (refs[:7], tables, w_q, w_s, w_up)

    @pl.when(pl.program_id(0) == 0)
    def _():
        sums[...] = jnp.zeros_like(sums)
        vecs[...] = jnp.zeros_like(vecs)

    x, g = pick(tokens, n, x_scr), pick(cots, n, g_scr)
    made = forward_part(x, *given, xh, act, qq, kk, vv)
    backward_part(g, scale, *made, w_down, w_out, sums, vecs, back, dd, ob)


def forward_kernel(n, pieces, place, *refs):
    tokens, refs = refs[: n * pieces], refs[n * pieces :]
    *tables, w_q, w_s, w_up = refs[7:12]
    xh, act, qq, kk, vv, slope, x_scr = refs[12 + 5 :]
    given = (refs[:7], tables, w_q, w_s, w_up)
    x = pick(tokens, n, x_scr)
    *_, made = forward_part(x, *given, xh, act, qq, kk, vv)
    slope[...] = made.astype(BF)


def backward_kernel(n, pieces, place, subset, weight, *refs):
    scale = weight[subset[0]]
    cots, refs = refs[: n * pieces], refs[n * pieces :]
    xh, act, slope, w_up, w_down, w_out, vecs_in, sums_in = refs[:8]
    sums_out, vecs, back, dd, ob, g_scr, sums = refs[8 + 3 :]
    step = pl.program_id(0)

    @pl.when(step == 0)
    def _():
        sums[...] = sums_in[...]
        vecs[...] = vecs_in[...]

    backward_part(
        pick(cots, n, g_scr),
        scale,
        xh[...],
        act[...],
        slope[...].astype(F32),
        w_down,
        w_out,
        sums,
        vecs,
        back,
        dd,
        ob,
    )

    @pl.when(step == pl.num_programs(0) - 1)
    def _():
        width = w_up.shape[0]
        sums_out[...] = sums[...].astype(BF)
        up_sum = sums[width:, :]
        up = w_up[...].astype(F32)
        gain_back = jnp.sum(up * up_sum, 1, keepdims=True)
        shift_back = jnp.sum(up * vecs[2:3, :], 1, keepdims=True)
        vecs[0:2, :] = as_rows(gain_back, shift_back)


def as_rows(first, second):
    lane = lax.broadcasted_iota(jnp.int32, (first.shape[0], LANES), 1)
    return jnp.where(lane == 0, first, second).T[:2, :]


def rows_call(kind, place, fixed, group_rows, scale=None, tokens=(), cots=(), carried=None, slope=None):
    n = place.shape[0]
    given = [*tokens, *cots]
    width = given[0].shape[1]
    rows = group_rows // fixed["parts"]
    hidden = fixed["w_up"].shape[1]
    anywhere = pl.BlockSpec(memory_space=pl.ANY)
    widths = {
        "xh": width,
        "act": hidden,
        "qq": 2 * LANES,
        "kk": LANES,
        "vv": LANES,
        "back": hidden,
        "dd": 2 * LANES,
        "ob": width,
    }
    sums_shape = (2 * width, hidden)

    def whole(shape):
        return pl.BlockSpec(shape, lambda i, place: (0,) * len(shape))

    def placed(columns):
        return pl.BlockSpec((rows, columns), lambda i, place: (place[i], 0))

    def in_turn(columns):
        return pl.BlockSpec((rows, columns), lambda i, place: (i, 0))

    args, in_specs = [], []
    kept_near = ("xh", "qq", "kk", "vv", "dd", "ob", "sums", "slope", "act", "back")

    def where(name):
        return near if name in kept_near else main_memory

    def take(arrays, specs):
        args.extend(arrays)
        in_specs.extend(specs)

    def full(*names):
        arrays = [near(fixed[k]) if k in ("w_up", "w_down") else fixed[k] for k in names]
        take(arrays, [whole(a.shape) for a in arrays])

    if scale is not None:
        take(scale, [pl.BlockSpec(memory_space=pltpu.SMEM)] * 2)
    take(given, [whole(a.shape) for a in given])
    outs, scratch = {}, []
    if kind == "backward":
        take([near(carried["xh"]), near(carried["act"])], [placed(width), placed(hidden)])
        take([near(slope)], [in_turn(hidden)])
        full("w_up", "w_down", "w_out")
        take([carried["vecs"], near(carried["sums"])], [whole((8, width)), whole(sums_shape)])
        names = ["back", "dd", "ob"]
        outs["sums"] = (sums_shape, BF, whole(sums_shape))
        outs["vecs"] = ((8, width), F32, whole((8, width)))
        scratch = [pltpu.VMEM((rows, width), BF)]
        scratch += [pltpu.VMEM(sums_shape, F32)]
    else:
        full(*VECTORS)
        take([near(t) for t in fixed["tables"]], [placed(LANES)] * 2)
        full("w_q", "w_s", "w_up")
        names = ["xh", "act", "qq", "kk", "vv"]
        scratch = [pltpu.VMEM((rows, width), BF)]
        if kind == "first":
            full("w_down", "w_out")
            names += ["back", "dd", "ob"]
            outs["sums"] = (sums_shape, F32, whole(sums_shape))
            outs["vecs"] = ((8, width), F32, whole((8, width)))
            scratch = scratch * 2
    aliases = {}
    for k in names:
        if carried is not None:
            aliases[len(args) + 1] = len(outs)
            take([where(k)(carried[k])], [anywhere])
        outs[k] = ((group_rows, widths[k]), BF, placed(widths[k]))
    if kind == "forward":
        outs["slope"] = ((n * rows, hidden), BF, in_turn(hidden))
    kernel = {
        "first": functools.partial(first_kernel, n),
        "forward": functools.partial(forward_kernel, n, len(tokens) // n),
        "backward": functools.partial(backward_kernel, n, len(cots) // n),
    }[kind]
    results = pl.pallas_call(
        kernel,
        grid_spec=pltpu.PrefetchScalarGridSpec(
            num_scalar_prefetch=1,
            grid=(n,),
            in_specs=in_specs,
            out_specs=[spec for *_, spec in outs.values()],
            scratch_shapes=scratch,
        ),
        out_shape=[
            (pltpu.VMEM if k in kept_near else pltpu.HBM)(shape, kind_)
            for k, (shape, kind_, _) in outs.items()
        ],
        input_output_aliases=aliases,
        compiler_params=pltpu.CompilerParams(vmem_limit_bytes=13 * 2**20),
        cost_estimate=pl.CostEstimate(
            flops=n * 4 * 10**8, bytes_accessed=2**20, transcendentals=0
        ),
        name=f"rows_{kind}",
    )(place, *args)
    return {**(carried or {}), **dict(zip(outs, results))}


def attention_kernel(block, first, final, parts, waits, *refs):
    qq, dd, kk, vv, cosine, sine, ob, xh = refs[:8]
    refs = refs[8:]
    if final:
        w_q, w_s, vecs = refs[:3]
        refs = refs[3:]
    refs = refs[waits:]
    if not first:
        carried = refs[:7]
        refs = refs[7 + 3 :]
    if not final:
        k_out, v_out, *sums_out = refs[:7]
        refs = refs[7:]
    context_out, query_out, shared_out = refs[:3]
    refs = refs[3:]
    if final:
        payload, shared_sum, vectors = refs[:3]
        refs = refs[3:]
    s_scr, d_scr, k_acc, v_acc = refs[:4]
    if final:
        sums_out = refs[4:]
    g_out, g_q, g_s, b_q, b_s = sums_out
    here = pl.ds(block * BLOCK, BLOCK)

    def add(which, value):
        sums_out[which][...] = value if first else carried[2 + which][...] + value

    def column_sum(a):
        return jnp.broadcast_to(jnp.sum(a.astype(F32), axis=0, keepdims=True), (8, a.shape[1]))

    left = lax.broadcasted_iota(jnp.int32, (BLOCK, LANES), 1) < HEAD_DIM
    zero = jnp.zeros((BLOCK, LANES), BF)

    def split(ref):
        pair, last = ref[:, :LANES], ref[:, LANES:]
        return jnp.where(left, pair, zero), jnp.where(left, zero, pair), last

    def lanes(s, op):
        out = s[:, :LANES]
        for j in range(1, BLOCK // LANES):
            out = op(out, s[:, j * LANES : (j + 1) * LANES])
        return out

    mixed, turned = [], []
    for head, (queries, incoming) in enumerate(zip(split(qq[here, :]), split(dd[here, :]))):
        queries = queries * jnp.asarray(HEAD_DIM**-0.5, BF)
        queries_t, incoming_t = queries.T, incoming.T
        slot = head % 2
        peak = None
        for t in range(block + 1):
            at = pl.ds(t * BLOCK, BLOCK)
            s = mm_cols(queries, kk[at, :])
            if t == block:
                key = lax.broadcasted_iota(jnp.int32, (BLOCK, BLOCK), 1)
                place = lax.broadcasted_iota(jnp.int32, (BLOCK, BLOCK), 0)
                s = jnp.where(key <= place, s, NEGATIVE)
            s_scr[slot, :, at] = s
            top = lanes(s, jnp.maximum)
            peak = top if peak is None else jnp.maximum(peak, top)
        peak = jnp.max(peak, axis=1, keepdims=True)

        total = centre = jnp.zeros((BLOCK, LANES), F32)
        out = None
        for t in range(block + 1):
            at = pl.ds(t * BLOCK, BLOCK)
            p = jnp.exp(s_scr[slot, :, at] - peak)
            d = mm_cols(incoming, vv[at, :])
            s_scr[slot, :, at] = p
            d_scr[slot, :, at] = d
            part = mm(p.astype(BF), vv[at, :])
            out = part if out is None else out + part
            total = total + lanes(p, jnp.add)
            centre = centre + lanes(p * d, jnp.add)
        inverse = 1.0 / jnp.sum(total, axis=1, keepdims=True)
        centre = jnp.sum(centre, axis=1, keepdims=True) * inverse
        mixed.append(out * inverse)

        out = None
        for t in range(block + 1):
            at = pl.ds(t * BLOCK, BLOCK)
            p = s_scr[slot, :, at] * inverse
            ds = (p * (d_scr[slot, :, at] - centre)).astype(BF)
            v_part = mm(incoming_t, p.astype(BF))
            k_part = mm(queries_t, ds)
            if head == 0 and first:
                v_acc[:, at] = v_part
                k_acc[:, at] = k_part
            elif head == 0:
                v_acc[:, at] = carried[1][:, at] + v_part
                k_acc[:, at] = carried[0][:, at] + k_part
            else:
                v_acc[:, at] += v_part
                k_acc[:, at] += k_part
            part = mm(ds, kk[at, :])
            out = part if out is None else out + part
        turned.append(out * HEAD_DIM**-0.5)
    if not final:
        k_out[...] = k_acc[:, : block * BLOCK]
        v_out[...] = v_acc[:, : block * BLOCK]

    def unstack(a):
        return jnp.where(left, a[0], a[1]), jnp.where(left, a[2], 0.0)

    c, s = cosine[here, :], sine[here, :]
    context = jnp.concatenate([a.astype(BF) for a in unstack(mixed)], 1)
    context_out[...] = context
    add(0, mm_rows(context, ob[here, :]))

    query_back = jnp.concatenate(
        [turn(a, c, s, -1.0).astype(BF) for a in unstack(turned)], 1
    )
    key_back = k_acc[:, here].T
    value_back = v_acc[:, here].T
    key_back = turn(key_back + pltpu.roll(key_back, HEAD_DIM, 1), c, s, -1.0)
    value_back = value_back + pltpu.roll(value_back, HEAD_DIM, 1)
    shared_back = jnp.where(left, key_back, value_back).astype(BF)
    xhat = xh[here, :]
    add(1, mm_rows(query_back, xhat))
    add(2, mm_rows(shared_back, xhat))
    add(3, column_sum(query_back))
    add(4, column_sum(shared_back))
    query_out[...] = query_back
    shared_out[...] = shared_back

    if final:
        wq, ws = w_q[...].astype(F32), w_s[...].astype(F32)
        local, width = wq.shape
        gq, gs = g_q[:local, :], g_s[...].T
        q_column = b_q[...].T[:local, 0:1]
        gain_row = jnp.sum(wq * gq, 0, keepdims=True)
        shift_row = jnp.sum(wq * q_column, 0, keepdims=True)
        shared_rows = as_rows(
            jnp.sum(ws * gs, 1, keepdims=True), jnp.sum(ws * b_s[0:1, :], 1, keepdims=True)
        )
        payload[:local, :] = gq.astype(BF)
        payload[local:, :] = g_out[:local, :].astype(BF)
        across = width // LANES
        third = width // parts // across
        for quarter in range(parts):
            for i in range(across):
                source = (across * quarter + i) * third
                shared_sum[
                    quarter * third : (quarter + 1) * third, i * LANES : (i + 1) * LANES
                ] = gs[source : source + third, :].astype(BF)
        zeros = jnp.zeros((1, width), F32)
        s_row = jnp.concatenate([b_s[0:1, :], zeros[:, LANES:]], 1)
        q_row = jnp.concatenate([b_q[0:1, :], zeros[:, 2 * LANES :]], 1)
        vectors[...] = jnp.concatenate(
            [
                gain_row + shared_rows[0:1, :],
                shift_row + shared_rows[1:2, :],
                vecs[0:2, :],
                s_row,
                vecs[2:4, :],
                q_row,
            ],
            0,
        )


def attention_call(block, made, vecs, fixed, final, waits=(), carried=None):
    qq, kk, vv, dd, xh, ob = made
    group_rows, width = xh.shape
    first = carried is None
    seen = (block + 1) * BLOCK

    def placed(columns):
        return pl.BlockSpec((BLOCK, columns), lambda i: (block, 0))

    def whole(shape):
        return pl.BlockSpec(shape, lambda i: (0,) * len(shape))

    anywhere = pl.BlockSpec(memory_space=pl.ANY)
    args = [near(a) for a in (qq, dd, kk, vv, *fixed["tables"], ob, xh)]
    in_specs = [whole(a.shape) for a in args]
    if final:
        full = [fixed["w_q"], fixed["w_s"], vecs]
        in_specs += [whole(a.shape) for a in full]
        args += full
    in_specs += [anywhere] * len(waits)
    args += list(waits)
    sums = [
        (2 * LANES, width),
        (2 * LANES, width),
        (LANES, width),
        (8, 2 * LANES),
        (8, LANES),
    ]
    shapes = [] if final else [(LANES, block * BLOCK)] * 2 + sums
    out_shape = [pltpu.VMEM(s, F32) for s in shapes]
    out_specs = [whole(s) for s in shapes]
    aliases = {}
    columns = [2 * LANES, 2 * LANES, LANES]
    if not first:
        start, at = len(args) + 7, len(shapes)
        in_specs += [whole(a.shape) for a in carried[:7]] + [anywhere] * 3
        args += [near(a) for a in carried]
        aliases = {start + i: at + i for i in range(3)}
    out_shape += [pltpu.VMEM((group_rows, c), BF) for c in columns]
    out_specs += [placed(c) for c in columns]
    if final:
        last = [((2 * fixed["w_q"].shape[0], width), BF), ((LANES, width), BF), ((8, width), F32)]
        out_shape += [jax.ShapeDtypeStruct(s, t) for s, t in last]
        out_specs += [whole(s) for s, _ in last]
    scratch = [
        pltpu.VMEM((2, BLOCK, seen), F32),
        pltpu.VMEM((2, BLOCK, seen), F32),
        pltpu.VMEM((LANES, seen), F32),
        pltpu.VMEM((LANES, seen), F32),
        *[pltpu.VMEM(s, F32) for s in (sums if final else [])],
    ]
    return pl.pallas_call(
        functools.partial(attention_kernel, block, first, final, fixed["parts"], len(waits)),
        grid=(1,),
        in_specs=in_specs,
        out_specs=out_specs,
        scratch_shapes=scratch,
        out_shape=out_shape,
        input_output_aliases=aliases,
        compiler_params=pltpu.CompilerParams(vmem_limit_bytes=(2 + 5 * (block + 1)) * 2**20),
        cost_estimate=pl.CostEstimate(
            flops=(block + 2) * 4 * 10**9, bytes_accessed=2**20, transcendentals=0
        ),
        name=f"attend{block}",
    )(*args)


def back_kernel(added, waits, place, *refs):
    act, back, context, query_back, shared_back = refs[:5]
    w_down, w_up, w_out, w_q, w_s, a_gain, f_gain = refs[5:12]
    refs = refs[12:]
    local = w_q.shape[0]
    branch = mm_cols(act[...], w_down[...]) + mm(context[:, :local], w_out[...])
    e = mm(query_back[:, :local], w_q[...]) + mm_cols(shared_back[...], w_s[...])
    w = e * line(a_gain) + mm_cols(back[...], w_up[...]) * line(f_gain)
    if added:
        branch = branch + refs[0][...].astype(F32)
        w = w + refs[1][...].astype(F32)
        refs = refs[2:]
    branch_out, w_out_ref = refs[waits:]
    branch_out[...] = branch.astype(branch_out.dtype)
    w_out_ref[...] = w.astype(w_out_ref.dtype)


def back_call(place, kept, fixed, own_rows, dtype, came=(), waits=()):
    width = kept[0].shape[1]

    def whole(a):
        return pl.BlockSpec(a.shape, lambda i, place: (0,) * a.ndim)

    full = [fixed[k] for k in ("w_down", "w_up", "w_out", "w_q", "w_s", "a_gain", "f_gain")] + list(came)
    in_specs = [
        pl.BlockSpec((own_rows, a.shape[1]), lambda i, place: (place[0], 0)) for a in kept
    ]
    in_specs += [whole(a) for a in full] + [pl.BlockSpec(memory_space=pl.ANY)] * len(waits)
    kept = [near(a) for a in kept]
    full = [near(a) for a in full[:2]] + full[2:]
    out = jax.ShapeDtypeStruct((own_rows, width), dtype)
    return pl.pallas_call(
        functools.partial(back_kernel, len(came) > 0, len(waits)),
        grid_spec=pltpu.PrefetchScalarGridSpec(
            num_scalar_prefetch=1,
            grid=(1,),
            in_specs=in_specs,
            out_specs=[pl.BlockSpec((own_rows, width), lambda i, place: (0, 0))] * 2,
        ),
        out_shape=[out, out],
        compiler_params=pltpu.CompilerParams(vmem_limit_bytes=10 * 2**20),
        cost_estimate=pl.CostEstimate(
            flops=8 * 10**9, bytes_accessed=2**20, transcendentals=0
        ),
        name="back",
    )(place, *kept, *full, *waits)


def swap(a, axis, bit):
    size = lax.axis_size(axis)
    return lax.ppermute(a, axis, [(i, i ^ bit) for i in range(size)])


def bits_of(size):
    return [1 << i for i in range(size.bit_length() - 1)]


def halving(a, axis, order):
    size = lax.axis_size(axis)
    index = lax.axis_index(axis)
    for bit in order:
        half = a.shape[0] // 2
        mine = (index // bit) % 2
        keep = lax.dynamic_slice_in_dim(a, mine * half, half, 0)
        send = lax.dynamic_slice_in_dim(a, (1 - mine) * half, half, 0)
        other = yield swap(send.astype(BF), axis, bit)
        a = keep.astype(F32) + other.astype(F32)
    return a


def doubling(a, axis, order):
    index = lax.axis_index(axis)
    a = a.astype(BF)
    for bit in order[::-1]:
        mine = (index // bit) % 2
        other = yield swap(a, axis, bit)
        first, second = jnp.where(mine == 0, a, other), jnp.where(mine == 0, other, a)
        a = jnp.concatenate([first, second], 0)
    return a


def summing(a, axis, order):
    a = yield from halving(a, axis, order)
    return (yield from doubling(a, axis, order))


class Chain:
    def __init__(self, steps):
        self.steps = steps
        self.waiting = next(steps)
        self.result = None

    def advance(self):
        try:
            self.waiting = self.steps.send(self.waiting)
        except StopIteration as stop:
            self.waiting, self.result = None, stop.value

    def finish(self):
        while self.waiting is not None:
            self.advance()
        return self.result


def together(chains, arrays=()):
    waiting, arrays = lax.optimization_barrier(([c.waiting for c in chains], list(arrays)))
    for chain, value in zip(chains, waiting):
        chain.waiting = value
    return arrays


def advance(chains):
    for chain in chains:
        if chain.waiting is not None:
            chain.advance()


def on_device(
    tokens,
    source_subset,
    subset_weight,
    output_cotangent,
    attention_gain,
    attention_shift,
    feed_gain,
    feed_shift,
    query_weight,
    query_bias,
    shared_weight,
    shared_bias,
    out_weight,
    up_weight,
    up_bias,
    down_weight,
    out_bias,
):
    own_rows, width = tokens.shape
    parts = lax.axis_size("tensor")
    group_rows = own_rows * parts
    me = lax.axis_index("tensor")

    half = own_rows // 2
    tok1 = swap(tokens, "tensor", 1)
    cot1 = swap(output_cotangent, "tensor", 1)
    tok2 = [swap(tokens[i * half : (i + 1) * half], "tensor", 2) for i in range(2)]
    cot2 = [swap(output_cotangent[i * half : (i + 1) * half], "tensor", 2) for i in range(2)]

    local = query_weight.shape[1]
    fixed = {
        "a_gain": attention_gain,
        "a_shift": attention_shift,
        "f_gain": feed_gain,
        "f_shift": feed_shift,
        "up_bias": up_bias,
        "q_bias": query_bias,
        "s_bias": shared_bias,
        "tables": rope_tables(),
        "w_up": up_weight,
        "w_down": down_weight,
        "w_out": out_weight.T,
        "w_q": query_weight.T,
        "w_s": shared_weight,
        "parts": parts,
    }
    scale_in = [source_subset, subset_weight]
    chunk = [(me ^ k).astype(jnp.int32) for k in range(parts)]
    made = rows_call(
        "first",
        jnp.stack(chunk[:2]),
        fixed,
        group_rows,
        scale_in,
        [tokens, tok1],
        [output_cotangent, cot1],
    )
    far_places = jnp.stack(chunk[2:])
    *tok2, cot2[0], made["xh"] = lax.optimization_barrier((*tok2, cot2[0], made["xh"]))
    tok3 = [swap(a, "tensor", 1) for a in tok2]
    cot3 = [swap(cot2[0], "tensor", 1)]
    made = rows_call(
        "forward", far_places, fixed, group_rows, None, tok2 + tok3, (), made
    )
    cot2[1], slope = lax.optimization_barrier((cot2[1], made.pop("slope")))
    cot3.append(swap(cot2[1], "tensor", 1))
    made = rows_call(
        "backward", far_places, fixed, group_rows, scale_in, (), cot2 + cot3, made, slope
    )
    sums, vecs, act, back = (made[k] for k in ("sums", "vecs", "act", "back"))
    made = [made[k] for k in ("qq", "kk", "vv", "dd", "xh", "ob")]

    bits = bits_of(lax.axis_size("batch"))
    turned_bits = bits[1:] + bits[:1]
    down_chain = Chain(summing(sums[:width], "batch", bits))
    up_chain = Chain(summing(sums[width:], "batch", turned_bits))
    carried, waits = None, ()
    for block in range(group_rows // BLOCK)[::-1]:
        final = block == 0
        carried = attention_call(block, made, vecs, fixed, final, waits, carried)
        waits = tuple(c.waiting for c in (down_chain, up_chain))
        if not final:
            advance((down_chain, up_chain))
    *kept, payload, shared_sum, vectors = carried
    kept = [act, back, *kept]

    small_rows = shared_sum.shape[0] // parts
    sent = [
        jnp.concatenate(
            [lax.dynamic_slice_in_dim(shared_sum, c * small_rows, small_rows, 0), vectors.astype(BF)],
            0,
        )
        for c in chunk
    ]
    others = [swap(sent[k], "tensor", k) for k in range(1, parts)]
    send3 = back_call(chunk[3].reshape(1), kept, fixed, own_rows, BF)
    got3 = [swap(a, "tensor", 1) for a in send3]
    send1 = back_call(chunk[1].reshape(1), kept, fixed, own_rows, BF, (), (*others,))
    got1 = [swap(a, "tensor", 1) for a in send1]
    own = jnp.concatenate([sent[0][:small_rows].astype(F32), vectors], 0)
    every = own
    for other in others:
        every = every + other.astype(F32)
    row = jnp.arange(small_rows + 8, dtype=jnp.int32)[:, None] - small_rows
    every = jnp.where(row >= 5, own, every)
    pieces = lax.axis_size("batch")
    columns = payload.shape[1]
    room = -(-every.shape[0] // (8 * pieces)) * 8 * pieces
    every = jnp.pad(every.astype(BF), ((0, room - every.shape[0]), (0, 0)))
    joined = jnp.concatenate(
        [payload.reshape(pieces, -1, columns), every.reshape(pieces, -1, columns)], 1
    )
    per_piece, main_rows = joined.shape[1], payload.shape[0] // pieces
    main = Chain(summing(joined.reshape(-1, columns), "batch", bits))
    gradients = (down_chain, up_chain)
    far = back_call(chunk[2].reshape(1), kept, fixed, own_rows, BF, got3)
    near = back_call(chunk[0].reshape(1), kept, fixed, own_rows, F32, got1)
    parts_y = [a[i * half : (i + 1) * half] for a in (far[1], far[0]) for i in range(2)]
    came = []
    w = near[1]
    for step in range(2 * len(bits) - 1):
        crossing = [swap(parts_y[step - 1], "tensor", 2)] if 0 < step <= len(parts_y) else []
        now = {0: (main, *gradients), 1: (main, down_chain), 3: (main, up_chain)}.get(step, (main,))
        if step == 4:
            w = near[1] + jnp.concatenate(came[:2], 0).astype(F32)
            xhat, inverse = normalize(tokens.astype(F32))
            tokens_back = output_cotangent.astype(F32) * subset_weight[source_subset[0]] + inverse * (
                w
                - jnp.mean(w, axis=-1, keepdims=True)
                - xhat * jnp.mean(w * xhat, axis=-1, keepdims=True)
            )
            tokens_back, *crossing = together(now, [tokens_back.astype(BF), *crossing])
        else:
            crossing = together(now, crossing)
        came += crossing
        advance(now)
    main.advance()
    joined = main.result.reshape(pieces, per_piece, columns)
    every = joined[:, main_rows:].reshape(-1, columns)
    payload = joined[:, :main_rows].reshape(-1, columns).astype(F32)
    shared_parts = [every[:small_rows]]
    shared_parts += [swap(every[:small_rows], "tensor", k) for k in range(1, parts)]
    vectors = every[small_rows : small_rows + 8]
    branch = near[0] + jnp.concatenate(came[2:], 0).astype(F32)
    mixed = (tokens.astype(F32) + branch + out_bias.astype(F32)).astype(BF)

    vectors = vectors.astype(F32)
    gain_back, shift_back, feed_gain_back, feed_shift_back, b_s, up_back, out_back, b_q = vectors
    b_s, b_q = b_s[: 2 * HEAD_DIM], b_q[:local]
    stacked = jnp.stack(shared_parts)
    ordered = jnp.stack([lax.dynamic_index_in_dim(stacked, me ^ j, 0, False) for j in range(parts)])
    g_s = jnp.swapaxes(ordered.reshape(parts, small_rows, width // LANES, LANES), 1, 2).reshape(-1, LANES)
    shared_back = g_s.astype(F32) * attention_gain[:, None] + attention_shift[:, None] * b_s[None, :]
    down_sum, up_sum = down_chain.finish(), up_chain.finish()
    query_back = payload[:local] * attention_gain[None, :]
    query_back = (query_back + b_q[:, None] * attention_shift[None, :]).T
    g_out = payload[local:].T
    up_back_matrix = up_sum.astype(F32) * feed_gain[:, None] + feed_shift[:, None] * up_back[None, :]
    return (
        mixed,
        tokens_back,
        gain_back,
        shift_back,
        feed_gain_back,
        feed_shift_back,
        query_back,
        b_q,
        shared_back,
        b_s,
        g_out,
        up_back_matrix,
        up_back,
        down_sum.astype(F32),
        out_back,
    )


def solution(mesh):
    return jax.shard_map(
        on_device,
        mesh=mesh,
        in_specs=(
            P(("batch", "tensor"), None),
            P("batch"),
            P(),
            P(("batch", "tensor"), None),
            P(),
            P(),
            P(),
            P(),
            P(None, "tensor"),
            P("tensor"),
            P(),
            P(),
            P(None, "tensor"),
            P(None, "tensor"),
            P("tensor"),
            P(None, "tensor"),
            P(),
        ),
        out_specs=(
            P(("batch", "tensor"), None),
            P(("batch", "tensor"), None),
            P(),
            P(),
            P(),
            P(),
            P(None, "tensor"),
            P("tensor"),
            P(),
            P(),
            P(None, "tensor"),
            P(None, "tensor"),
            P("tensor"),
            P(None, "tensor"),
            P(),
        ),
        check_vma=False,
    )
```

```python
import functools

import jax
import jax.numpy as jnp
import numpy as np
from jax import lax
from jax.experimental import pallas as pl
from jax.experimental.pallas import tpu as pltpu
from jax.sharding import PartitionSpec as P

HEAD_DIM = 64
LEN = 2048
ROT = 16
HALF = ROT // 2
BLOCK = 512
LANES = 128
VECTORS = ("a_gain", "a_shift", "f_gain", "f_shift", "up_bias", "q_bias", "s_bias")

EPSILON = 1e-05
NEGATIVE = -1e30
BF = jnp.bfloat16
F32 = jnp.float32


def near(a):
    return pltpu.with_memory_space_constraint(a, pltpu.VMEM)


def main_memory(a):
    return pltpu.with_memory_space_constraint(a, pltpu.HBM)


def mm(left, right):
    return jnp.dot(left, right, preferred_element_type=F32)


def mm_rows(left, right):
    return lax.dot_general(left, right, (((0,), (0,)), ((), ())), preferred_element_type=F32)


def mm_cols(left, right):
    return lax.dot_general(left, right, (((1,), (1,)), ((), ())), preferred_element_type=F32)


def rope_tables():
    lane = np.arange(LANES) % HEAD_DIM
    frequency = (10000.0 ** (-2.0 * np.arange(HALF, dtype=np.float32) / ROT)).astype(np.float32)
    angles = np.arange(LEN, dtype=np.float32)[:, None] * frequency[lane % HALF][None, :]
    angles = angles.astype(np.float32).astype(np.float64)
    turned = lane < ROT
    cosine = np.where(turned, np.cos(angles), 1.0)
    sine = np.where(lane < HALF, -np.sin(angles), np.where(turned, np.sin(angles), 0.0))
    return [jnp.asarray(t.astype(np.float32)) for t in (cosine, sine)]


def turn(values, cosine, sine, sign):
    lane = lax.broadcasted_iota(jnp.int32, values.shape, 1)
    up = pltpu.roll(values, LANES - HALF, 1)
    down = pltpu.roll(values, HALF, 1)
    return values * cosine + sign * sine * jnp.where(lane % HEAD_DIM < HALF, up, down)


def normalize(rows):
    centred = rows - jnp.mean(rows, axis=-1, keepdims=True)
    variance = jnp.mean(centred * centred, axis=-1, keepdims=True)
    scale = lax.rsqrt(variance + EPSILON)
    return centred * scale, scale


def pick(refs, scratch):
    rows = scratch.shape[0]
    start = 0
    for ref in refs:
        part, at = divmod(start, rows)
        start += ref.shape[0]

        @pl.when(pl.program_id(0) == part)
        def _(ref=ref, at=at):
            scratch[at : at + ref.shape[0], :] = ref[...]

    return scratch[...]


def two_slabs(a):
    rest = a[:, LANES:]
    filler = jnp.zeros((a.shape[0], 2 * LANES - a.shape[1]), a.dtype)
    return a[:, :LANES], jnp.concatenate([rest, filler], 1)


def line(ref):
    return ref[...].astype(F32)[None, :]


def forward_part(x, vectors, tables, w_q, w_s, w_up, xh, act, qq, kk, vv):
    xhat, _ = normalize(x.astype(F32))
    xhat_low = xhat.astype(BF)
    xh[...] = xhat_low
    a_gain, a_shift, f_gain, f_shift, up_bias, q_bias, s_bias = (line(v) for v in vectors)
    attention_in = (xhat * a_gain + a_shift).astype(BF)
    feed_in = (xhat * f_gain + f_shift).astype(BF)
    hidden = mm(feed_in, w_up[...]) + up_bias
    raw = mm_cols(attention_in, w_q[...]) + q_bias
    shared = mm(attention_in, w_s[...]) + s_bias
    cdf = 0.5 + 0.5 * lax.erf(hidden * (0.5**0.5))
    slope = cdf + hidden * (jnp.exp(-0.5 * hidden * hidden) * (2.0 * np.pi) ** -0.5)
    activated = (hidden * cdf).astype(BF)
    act[...] = activated
    c, s = (t[...] for t in tables)
    pair, last = two_slabs(raw)
    qq[:, :LANES] = turn(pair, c, s, 1.0).astype(BF)
    qq[:, LANES:] = turn(last, c, s, 1.0).astype(BF)
    left = lax.broadcasted_iota(jnp.int32, shared.shape, 1) < HEAD_DIM
    twin = pltpu.roll(shared, HEAD_DIM, 1)
    kk[...] = turn(jnp.where(left, shared, twin), c, s, 1.0).astype(BF)
    vv[...] = jnp.where(left, twin, shared).astype(BF)
    return xhat_low, activated, slope


def backward_part(g, scale, xhat_low, activated, slope, w_down, w_out, sums, vecs, back, dd, ob):
    width = g.shape[1]
    outer = g.astype(F32) * scale
    outer_low = outer.astype(BF)
    ob[...] = outer_low
    vecs[3:4, :] += jnp.sum(outer, axis=0, keepdims=True)
    hidden_back = (mm(outer_low, w_down[...]) * slope).astype(BF)
    back[...] = hidden_back
    pair, last = two_slabs(mm_cols(outer_low, w_out[...]))
    dd[:, :LANES] = pair.astype(BF)
    dd[:, LANES:] = last.astype(BF)
    sums[:width, :] += mm_rows(outer_low, activated)
    sums[width:, :] += mm_rows(xhat_low, hidden_back)
    vecs[2:3, :] += jnp.sum(hidden_back.astype(F32), axis=0, keepdims=True)


def first_kernel(n, place, subset, weight, *refs):
    scale = weight[subset[0]]
    tokens, cots, refs = refs[:n], refs[n : 2 * n], refs[2 * n :]
    *tables, w_q, w_s, w_up, w_down, w_out = refs[7:14]
    sums, vecs, xh, act, qq, kk, vv, back, dd, ob, x_scr, g_scr = refs[14:]
    given = (refs[:7], tables, w_q, w_s, w_up)

    @pl.when(pl.program_id(0) == 0)
    def _():
        sums[...] = jnp.zeros_like(sums)
        vecs[...] = jnp.zeros_like(vecs)

    x, g = pick(tokens, x_scr), pick(cots, g_scr)
    made = forward_part(x, *given, xh, act, qq, kk, vv)
    backward_part(g, scale, *made, w_down, w_out, sums, vecs, back, dd, ob)


def forward_kernel(n, place, *refs):
    tokens, refs = refs[:n], refs[n:]
    *tables, w_q, w_s, w_up = refs[7:12]
    xh, act, qq, kk, vv, slope, x_scr = refs[12 + 5 :]
    given = (refs[:7], tables, w_q, w_s, w_up)
    x = pick(tokens, x_scr)
    *_, made = forward_part(x, *given, xh, act, qq, kk, vv)
    slope[...] = made.astype(BF)


def backward_kernel(n, place, subset, weight, *refs):
    scale = weight[subset[0]]
    cots, refs = refs[:n], refs[n:]
    xh, act, slope, w_up, w_down, w_out, vecs_in, sums_in = refs[:8]
    sums_out, vecs, back, dd, ob, g_scr, sums = refs[8 + 3 :]
    step = pl.program_id(0)

    @pl.when(step == 0)
    def _():
        sums[...] = sums_in[...]
        vecs[...] = vecs_in[...]

    backward_part(
        pick(cots, g_scr),
        scale,
        xh[...],
        act[...],
        slope[...].astype(F32),
        w_down,
        w_out,
        sums,
        vecs,
        back,
        dd,
        ob,
    )

    @pl.when(step == pl.num_programs(0) - 1)
    def _():
        width = w_up.shape[0]
        sums_out[...] = sums[...].astype(BF)
        up_sum = sums[width:, :]
        up = w_up[...].astype(F32)
        gain_back = jnp.sum(up * up_sum, 1, keepdims=True)
        shift_back = jnp.sum(up * vecs[2:3, :], 1, keepdims=True)
        vecs[0:2, :] = as_rows(gain_back, shift_back)


def as_rows(first, second):
    lane = lax.broadcasted_iota(jnp.int32, (first.shape[0], LANES), 1)
    return jnp.where(lane == 0, first, second).T[:2, :]


def rows_call(kind, place, fixed, group_rows, scale=None, tokens=(), cots=(), carried=None, slope=None):
    n = place.shape[0]
    given = [*tokens, *cots]
    width = given[0].shape[1]
    rows = group_rows // fixed["parts"]
    hidden = fixed["w_up"].shape[1]
    anywhere = pl.BlockSpec(memory_space=pl.ANY)
    widths = {
        "xh": width,
        "act": hidden,
        "qq": 2 * LANES,
        "kk": LANES,
        "vv": LANES,
        "back": hidden,
        "dd": 2 * LANES,
        "ob": width,
    }
    sums_shape = (2 * width, hidden)

    def whole(shape):
        return pl.BlockSpec(shape, lambda i, place: (0,) * len(shape))

    def placed(columns):
        return pl.BlockSpec((rows, columns), lambda i, place: (place[i], 0))

    def in_turn(columns):
        return pl.BlockSpec((rows, columns), lambda i, place: (i, 0))

    args, in_specs = [], []
    kept_near = ("xh", "qq", "kk", "vv", "dd", "ob", "sums", "slope", "act", "back")

    def where(name):
        return near if name in kept_near else main_memory

    def take(arrays, specs):
        args.extend(arrays)
        in_specs.extend(specs)

    def full(*names):
        arrays = [near(fixed[k]) if k in ("w_up", "w_down") else fixed[k] for k in names]
        take(arrays, [whole(a.shape) for a in arrays])

    if scale is not None:
        take(scale, [pl.BlockSpec(memory_space=pltpu.SMEM)] * 2)
    take(given, [whole(a.shape) for a in given])
    outs, scratch = {}, []
    if kind == "backward":
        take([near(carried["xh"]), near(carried["act"])], [placed(width), placed(hidden)])
        take([near(slope)], [in_turn(hidden)])
        full("w_up", "w_down", "w_out")
        take([carried["vecs"], near(carried["sums"])], [whole((8, width)), whole(sums_shape)])
        names = ["back", "dd", "ob"]
        outs["sums"] = (sums_shape, BF, whole(sums_shape))
        outs["vecs"] = ((8, width), F32, whole((8, width)))
        scratch = [pltpu.VMEM((rows, width), BF)]
        scratch += [pltpu.VMEM(sums_shape, F32)]
    else:
        full(*VECTORS)
        take([near(t) for t in fixed["tables"]], [placed(LANES)] * 2)
        full("w_q", "w_s", "w_up")
        names = ["xh", "act", "qq", "kk", "vv"]
        scratch = [pltpu.VMEM((rows, width), BF)]
        if kind == "first":
            full("w_down", "w_out")
            names += ["back", "dd", "ob"]
            outs["sums"] = (sums_shape, F32, whole(sums_shape))
            outs["vecs"] = ((8, width), F32, whole((8, width)))
            scratch = scratch * 2
    aliases = {}
    for k in names:
        if carried is not None:
            aliases[len(args) + 1] = len(outs)
            take([where(k)(carried[k])], [anywhere])
        outs[k] = ((group_rows, widths[k]), BF, placed(widths[k]))
    if kind == "forward":
        outs["slope"] = ((n * rows, hidden), BF, in_turn(hidden))
    kernel = {
        "first": functools.partial(first_kernel, n),
        "forward": functools.partial(forward_kernel, len(tokens)),
        "backward": functools.partial(backward_kernel, len(cots)),
    }[kind]
    results = pl.pallas_call(
        kernel,
        grid_spec=pltpu.PrefetchScalarGridSpec(
            num_scalar_prefetch=1,
            grid=(n,),
            in_specs=in_specs,
            out_specs=[spec for *_, spec in outs.values()],
            scratch_shapes=scratch,
        ),
        out_shape=[
            (pltpu.VMEM if k in kept_near else pltpu.HBM)(shape, kind_)
            for k, (shape, kind_, _) in outs.items()
        ],
        input_output_aliases=aliases,
        compiler_params=pltpu.CompilerParams(vmem_limit_bytes=13 * 2**20),
        cost_estimate=pl.CostEstimate(
            flops=n * 4 * 10**8, bytes_accessed=2**20, transcendentals=0
        ),
        name=f"rows_{kind}",
    )(place, *args)
    return {**(carried or {}), **dict(zip(outs, results))}


def attention_kernel(block, first, final, parts, waits, *refs):
    qq, dd, kk, vv, cosine, sine, ob, xh = refs[:8]
    refs = refs[8:]
    if final:
        w_q, w_s, vecs = refs[:3]
        refs = refs[3:]
    refs = refs[waits:]
    if not first:
        carried = refs[:7]
        refs = refs[7 + 3 :]
    if not final:
        k_out, v_out, *sums_out = refs[:7]
        refs = refs[7:]
    context_out, query_out, shared_out = refs[:3]
    refs = refs[3:]
    if final:
        payload, shared_sum, vectors = refs[:3]
        refs = refs[3:]
    s_scr, d_scr, k_acc, v_acc = refs[:4]
    if final:
        sums_out = refs[4:]
    g_out, g_q, g_s, b_q, b_s = sums_out
    here = pl.ds(block * BLOCK, BLOCK)

    def add(which, value):
        sums_out[which][...] = value if first else carried[2 + which][...] + value

    def column_sum(a):
        return jnp.broadcast_to(jnp.sum(a.astype(F32), axis=0, keepdims=True), (8, a.shape[1]))

    left = lax.broadcasted_iota(jnp.int32, (BLOCK, LANES), 1) < HEAD_DIM
    zero = jnp.zeros((BLOCK, LANES), BF)

    def split(ref):
        pair, last = ref[:, :LANES], ref[:, LANES:]
        return jnp.where(left, pair, zero), jnp.where(left, zero, pair), last

    def lanes(s, op):
        out = s[:, :LANES]
        for j in range(1, BLOCK // LANES):
            out = op(out, s[:, j * LANES : (j + 1) * LANES])
        return out

    mixed, turned = [], []
    for head, (queries, incoming) in enumerate(zip(split(qq[here, :]), split(dd[here, :]))):
        queries = queries * jnp.asarray(HEAD_DIM**-0.5, BF)
        queries_t, incoming_t = queries.T, incoming.T
        slot = head % 2
        peak = None
        for t in range(block + 1):
            at = pl.ds(t * BLOCK, BLOCK)
            s = mm_cols(queries, kk[at, :])
            if t == block:
                key = lax.broadcasted_iota(jnp.int32, (BLOCK, BLOCK), 1)
                place = lax.broadcasted_iota(jnp.int32, (BLOCK, BLOCK), 0)
                s = jnp.where(key <= place, s, NEGATIVE)
            s_scr[slot, :, at] = s
            top = lanes(s, jnp.maximum)
            peak = top if peak is None else jnp.maximum(peak, top)
        peak = jnp.max(peak, axis=1, keepdims=True)

        total = centre = jnp.zeros((BLOCK, LANES), F32)
        out = None
        for t in range(block + 1):
            at = pl.ds(t * BLOCK, BLOCK)
            p = jnp.exp(s_scr[slot, :, at] - peak)
            d = mm_cols(incoming, vv[at, :])
            s_scr[slot, :, at] = p
            d_scr[slot, :, at] = d
            part = mm(p.astype(BF), vv[at, :])
            out = part if out is None else out + part
            total = total + lanes(p, jnp.add)
            centre = centre + lanes(p * d, jnp.add)
        inverse = 1.0 / jnp.sum(total, axis=1, keepdims=True)
        centre = jnp.sum(centre, axis=1, keepdims=True) * inverse
        mixed.append(out * inverse)

        out = None
        for t in range(block + 1):
            at = pl.ds(t * BLOCK, BLOCK)
            p = s_scr[slot, :, at] * inverse
            ds = (p * (d_scr[slot, :, at] - centre)).astype(BF)
            v_part = mm(incoming_t, p.astype(BF))
            k_part = mm(queries_t, ds)
            if head == 0 and first:
                v_acc[:, at] = v_part
                k_acc[:, at] = k_part
            elif head == 0:
                v_acc[:, at] = carried[1][:, at] + v_part
                k_acc[:, at] = carried[0][:, at] + k_part
            else:
                v_acc[:, at] += v_part
                k_acc[:, at] += k_part
            part = mm(ds, kk[at, :])
            out = part if out is None else out + part
        turned.append(out * HEAD_DIM**-0.5)
    if not final:
        k_out[...] = k_acc[:, : block * BLOCK]
        v_out[...] = v_acc[:, : block * BLOCK]

    def unstack(a):
        return jnp.where(left, a[0], a[1]), jnp.where(left, a[2], 0.0)

    c, s = cosine[here, :], sine[here, :]
    context = jnp.concatenate([a.astype(BF) for a in unstack(mixed)], 1)
    context_out[...] = context
    add(0, mm_rows(context, ob[here, :]))

    query_back = jnp.concatenate(
        [turn(a, c, s, -1.0).astype(BF) for a in unstack(turned)], 1
    )
    key_back = k_acc[:, here].T
    value_back = v_acc[:, here].T
    key_back = turn(key_back + pltpu.roll(key_back, HEAD_DIM, 1), c, s, -1.0)
    value_back = value_back + pltpu.roll(value_back, HEAD_DIM, 1)
    shared_back = jnp.where(left, key_back, value_back).astype(BF)
    xhat = xh[here, :]
    add(1, mm_rows(query_back, xhat))
    add(2, mm_rows(shared_back, xhat))
    add(3, column_sum(query_back))
    add(4, column_sum(shared_back))
    query_out[...] = query_back
    shared_out[...] = shared_back

    if final:
        wq, ws = w_q[...].astype(F32), w_s[...].astype(F32)
        local, width = wq.shape
        gq, gs = g_q[:local, :], g_s[...].T
        q_column = b_q[...].T[:local, 0:1]
        gain_row = jnp.sum(wq * gq, 0, keepdims=True)
        shift_row = jnp.sum(wq * q_column, 0, keepdims=True)
        shared_rows = as_rows(
            jnp.sum(ws * gs, 1, keepdims=True), jnp.sum(ws * b_s[0:1, :], 1, keepdims=True)
        )
        payload[:local, :] = gq.astype(BF)
        payload[local:, :] = g_out[:local, :].astype(BF)
        across = width // LANES
        third = width // parts // across
        for quarter in range(parts):
            for i in range(across):
                source = (across * quarter + i) * third
                shared_sum[
                    quarter * third : (quarter + 1) * third, i * LANES : (i + 1) * LANES
                ] = gs[source : source + third, :].astype(BF)
        zeros = jnp.zeros((1, width), F32)
        s_row = jnp.concatenate([b_s[0:1, :], zeros[:, LANES:]], 1)
        q_row = jnp.concatenate([b_q[0:1, :], zeros[:, 2 * LANES :]], 1)
        vectors[...] = jnp.concatenate(
            [
                gain_row + shared_rows[0:1, :],
                shift_row + shared_rows[1:2, :],
                vecs[0:2, :],
                s_row,
                vecs[2:4, :],
                q_row,
            ],
            0,
        )


def attention_call(block, made, vecs, fixed, final, waits=(), carried=None):
    qq, kk, vv, dd, xh, ob = made
    group_rows, width = xh.shape
    first = carried is None
    seen = (block + 1) * BLOCK

    def placed(columns):
        return pl.BlockSpec((BLOCK, columns), lambda i: (block, 0))

    def whole(shape):
        return pl.BlockSpec(shape, lambda i: (0,) * len(shape))

    anywhere = pl.BlockSpec(memory_space=pl.ANY)
    args = [near(a) for a in (qq, dd, kk, vv, *fixed["tables"], ob, xh)]
    in_specs = [whole(a.shape) for a in args]
    if final:
        full = [fixed["w_q"], fixed["w_s"], vecs]
        in_specs += [whole(a.shape) for a in full]
        args += full
    in_specs += [anywhere] * len(waits)
    args += list(waits)
    sums = [
        (2 * LANES, width),
        (2 * LANES, width),
        (LANES, width),
        (8, 2 * LANES),
        (8, LANES),
    ]
    shapes = [] if final else [(LANES, block * BLOCK)] * 2 + sums
    out_shape = [pltpu.VMEM(s, F32) for s in shapes]
    out_specs = [whole(s) for s in shapes]
    aliases = {}
    columns = [2 * LANES, 2 * LANES, LANES]
    if not first:
        start, at = len(args) + 7, len(shapes)
        in_specs += [whole(a.shape) for a in carried[:7]] + [anywhere] * 3
        args += [near(a) for a in carried]
        aliases = {start + i: at + i for i in range(3)}
    out_shape += [pltpu.VMEM((group_rows, c), BF) for c in columns]
    out_specs += [placed(c) for c in columns]
    if final:
        last = [((2 * fixed["w_q"].shape[0], width), BF), ((LANES, width), BF), ((8, width), F32)]
        out_shape += [jax.ShapeDtypeStruct(s, t) for s, t in last]
        out_specs += [whole(s) for s, _ in last]
    scratch = [
        pltpu.VMEM((2, BLOCK, seen), F32),
        pltpu.VMEM((2, BLOCK, seen), F32),
        pltpu.VMEM((LANES, seen), F32),
        pltpu.VMEM((LANES, seen), F32),
        *[pltpu.VMEM(s, F32) for s in (sums if final else [])],
    ]
    return pl.pallas_call(
        functools.partial(attention_kernel, block, first, final, fixed["parts"], len(waits)),
        grid=(1,),
        in_specs=in_specs,
        out_specs=out_specs,
        scratch_shapes=scratch,
        out_shape=out_shape,
        input_output_aliases=aliases,
        compiler_params=pltpu.CompilerParams(vmem_limit_bytes=(2 + 5 * (block + 1)) * 2**20),
        cost_estimate=pl.CostEstimate(
            flops=(block + 2) * 4 * 10**9, bytes_accessed=2**20, transcendentals=0
        ),
        name=f"attend{block}",
    )(*args)


def back_kernel(added, waits, place, *refs):
    act, back, context, query_back, shared_back = refs[:5]
    w_down, w_up, w_out, w_q, w_s, a_gain, f_gain = refs[5:12]
    refs = refs[12:]
    local = w_q.shape[0]
    branch = mm_cols(act[...], w_down[...]) + mm(context[:, :local], w_out[...])
    e = mm(query_back[:, :local], w_q[...]) + mm_cols(shared_back[...], w_s[...])
    w = e * line(a_gain) + mm_cols(back[...], w_up[...]) * line(f_gain)
    if added:
        branch = branch + refs[0][...].astype(F32)
        w = w + refs[1][...].astype(F32)
        refs = refs[2:]
    branch_out, w_out_ref = refs[waits:]
    branch_out[...] = branch.astype(branch_out.dtype)
    w_out_ref[...] = w.astype(w_out_ref.dtype)


def back_call(place, kept, fixed, own_rows, dtype, came=(), waits=()):
    width = kept[0].shape[1]

    def whole(a):
        return pl.BlockSpec(a.shape, lambda i, place: (0,) * a.ndim)

    full = [fixed[k] for k in ("w_down", "w_up", "w_out", "w_q", "w_s", "a_gain", "f_gain")] + list(came)
    in_specs = [
        pl.BlockSpec((own_rows, a.shape[1]), lambda i, place: (place[0], 0)) for a in kept
    ]
    in_specs += [whole(a) for a in full] + [pl.BlockSpec(memory_space=pl.ANY)] * len(waits)
    kept = [near(a) for a in kept]
    full = [near(a) for a in full[:2]] + full[2:]
    out = jax.ShapeDtypeStruct((own_rows, width), dtype)
    return pl.pallas_call(
        functools.partial(back_kernel, len(came) > 0, len(waits)),
        grid_spec=pltpu.PrefetchScalarGridSpec(
            num_scalar_prefetch=1,
            grid=(1,),
            in_specs=in_specs,
            out_specs=[pl.BlockSpec((own_rows, width), lambda i, place: (0, 0))] * 2,
        ),
        out_shape=[out, out],
        compiler_params=pltpu.CompilerParams(vmem_limit_bytes=10 * 2**20),
        cost_estimate=pl.CostEstimate(
            flops=8 * 10**9, bytes_accessed=2**20, transcendentals=0
        ),
        name="back",
    )(place, *kept, *full, *waits)


def swap(a, axis, bit):
    size = lax.axis_size(axis)
    return lax.ppermute(a, axis, [(i, i ^ bit) for i in range(size)])


def bits_of(size):
    return [1 << i for i in range(size.bit_length() - 1)]


def halving(a, axis, order):
    size = lax.axis_size(axis)
    index = lax.axis_index(axis)
    for bit in order:
        half = a.shape[0] // 2
        mine = (index // bit) % 2
        keep = lax.dynamic_slice_in_dim(a, mine * half, half, 0)
        send = lax.dynamic_slice_in_dim(a, (1 - mine) * half, half, 0)
        other = yield swap(send.astype(BF), axis, bit)
        a = keep.astype(F32) + other.astype(F32)
    return a


def doubling(a, axis, order):
    index = lax.axis_index(axis)
    a = a.astype(BF)
    for bit in order[::-1]:
        mine = (index // bit) % 2
        other = yield swap(a, axis, bit)
        first, second = jnp.where(mine == 0, a, other), jnp.where(mine == 0, other, a)
        a = jnp.concatenate([first, second], 0)
    return a


def summing(a, axis, order):
    a = yield from halving(a, axis, order)
    return (yield from doubling(a, axis, order))


class Chain:
    def __init__(self, steps):
        self.steps = steps
        self.waiting = next(steps)
        self.result = None

    def advance(self):
        try:
            self.waiting = self.steps.send(self.waiting)
        except StopIteration as stop:
            self.waiting, self.result = None, stop.value

    def finish(self):
        while self.waiting is not None:
            self.advance()
        return self.result


def together(chains, arrays=()):
    waiting, arrays = lax.optimization_barrier(([c.waiting for c in chains], list(arrays)))
    for chain, value in zip(chains, waiting):
        chain.waiting = value
    return arrays


def advance(chains):
    for chain in chains:
        if chain.waiting is not None:
            chain.advance()


def on_device(
    tokens,
    source_subset,
    subset_weight,
    output_cotangent,
    attention_gain,
    attention_shift,
    feed_gain,
    feed_shift,
    query_weight,
    query_bias,
    shared_weight,
    shared_bias,
    out_weight,
    up_weight,
    up_bias,
    down_weight,
    out_bias,
):
    own_rows, width = tokens.shape
    parts = lax.axis_size("tensor")
    group_rows = own_rows * parts
    me = lax.axis_index("tensor")

    half = own_rows // 2
    tok1 = swap(tokens, "tensor", 1)
    cot1 = swap(output_cotangent, "tensor", 1)
    tok2 = swap(tokens, "tensor", 2)
    cot2 = [swap(output_cotangent[i * half : (i + 1) * half], "tensor", 2) for i in range(2)]

    local = query_weight.shape[1]
    fixed = {
        "a_gain": attention_gain,
        "a_shift": attention_shift,
        "f_gain": feed_gain,
        "f_shift": feed_shift,
        "up_bias": up_bias,
        "q_bias": query_bias,
        "s_bias": shared_bias,
        "tables": rope_tables(),
        "w_up": up_weight,
        "w_down": down_weight,
        "w_out": out_weight.T,
        "w_q": query_weight.T,
        "w_s": shared_weight,
        "parts": parts,
    }
    scale_in = [source_subset, subset_weight]
    chunk = [(me ^ k).astype(jnp.int32) for k in range(parts)]
    made = rows_call(
        "first",
        jnp.stack(chunk[:2]),
        fixed,
        group_rows,
        scale_in,
        [tokens, tok1],
        [output_cotangent, cot1],
    )
    far_places = jnp.stack(chunk[2:])
    tok2, cot2[0], made["xh"] = lax.optimization_barrier((tok2, cot2[0], made["xh"]))
    tok3 = [swap(tok2[i * half : (i + 1) * half], "tensor", 1) for i in range(2)]
    cot3 = [swap(cot2[0], "tensor", 1)]
    made = rows_call(
        "forward", far_places, fixed, group_rows, None, [tok2, *tok3], (), made
    )
    cot2[1], slope = lax.optimization_barrier((cot2[1], made.pop("slope")))
    cot3.append(swap(cot2[1], "tensor", 1))
    made = rows_call(
        "backward", far_places, fixed, group_rows, scale_in, (), cot2 + cot3, made, slope
    )
    sums, vecs, act, back = (made[k] for k in ("sums", "vecs", "act", "back"))
    made = [made[k] for k in ("qq", "kk", "vv", "dd", "xh", "ob")]

    bits = bits_of(lax.axis_size("batch"))
    turned_bits = bits[1:] + bits[:1]
    down_chain = Chain(summing(sums[:width], "batch", bits))
    up_chain = Chain(summing(sums[width:], "batch", turned_bits))
    carried, waits = None, ()
    for block in range(group_rows // BLOCK)[::-1]:
        final = block == 0
        carried = attention_call(block, made, vecs, fixed, final, waits, carried)
        waits = tuple(c.waiting for c in (down_chain, up_chain))
        if not final:
            advance((down_chain, up_chain))
    *kept, payload, shared_sum, vectors = carried
    kept = [act, back, *kept]

    small_rows = shared_sum.shape[0] // parts
    sent = [
        jnp.concatenate(
            [lax.dynamic_slice_in_dim(shared_sum, c * small_rows, small_rows, 0), vectors.astype(BF)],
            0,
        )
        for c in chunk
    ]
    others = [swap(sent[k], "tensor", k) for k in range(1, parts)]
    send3 = back_call(chunk[3].reshape(1), kept, fixed, own_rows, BF)
    got3 = [swap(a, "tensor", 1) for a in send3]
    send1 = back_call(chunk[1].reshape(1), kept, fixed, own_rows, BF, (), (*others,))
    got1 = [swap(a, "tensor", 1) for a in send1]
    own = jnp.concatenate([sent[0][:small_rows].astype(F32), vectors], 0)
    every = own
    for other in others:
        every = every + other.astype(F32)
    row = jnp.arange(small_rows + 8, dtype=jnp.int32)[:, None] - small_rows
    every = jnp.where(row >= 5, own, every)
    pieces = lax.axis_size("batch")
    columns = payload.shape[1]
    room = -(-every.shape[0] // (8 * pieces)) * 8 * pieces
    every = jnp.pad(every.astype(BF), ((0, room - every.shape[0]), (0, 0)))
    joined = jnp.concatenate(
        [payload.reshape(pieces, -1, columns), every.reshape(pieces, -1, columns)], 1
    )
    per_piece, main_rows = joined.shape[1], payload.shape[0] // pieces
    main = Chain(summing(joined.reshape(-1, columns), "batch", bits))
    gradients = (down_chain, up_chain)
    far = back_call(chunk[2].reshape(1), kept, fixed, own_rows, BF, got3)
    near = back_call(chunk[0].reshape(1), kept, fixed, own_rows, F32, got1)
    parts_y = [a[i * half : (i + 1) * half] for a in (far[1], far[0]) for i in range(2)]
    came = []
    w = near[1]
    for step in range(2 * len(bits) - 1):
        crossing = [swap(parts_y[step - 1], "tensor", 2)] if 0 < step <= len(parts_y) else []
        now = {0: (main, *gradients), 1: (main, down_chain), 3: (main, up_chain)}.get(step, (main,))
        if step == 4:
            w = near[1] + jnp.concatenate(came[:2], 0).astype(F32)
            xhat, inverse = normalize(tokens.astype(F32))
            tokens_back = output_cotangent.astype(F32) * subset_weight[source_subset[0]] + inverse * (
                w
                - jnp.mean(w, axis=-1, keepdims=True)
                - xhat * jnp.mean(w * xhat, axis=-1, keepdims=True)
            )
            tokens_back, *crossing = together(now, [tokens_back.astype(BF), *crossing])
        else:
            crossing = together(now, crossing)
        came += crossing
        advance(now)
    main.advance()
    joined = main.result.reshape(pieces, per_piece, columns)
    every = joined[:, main_rows:].reshape(-1, columns)
    payload = joined[:, :main_rows].reshape(-1, columns).astype(F32)
    shared_parts = [every[:small_rows]]
    shared_parts += [swap(every[:small_rows], "tensor", k) for k in range(1, parts)]
    vectors = every[small_rows : small_rows + 8]
    branch = near[0] + jnp.concatenate(came[2:], 0).astype(F32)
    mixed = (tokens.astype(F32) + branch + out_bias.astype(F32)).astype(BF)

    vectors = vectors.astype(F32)
    gain_back, shift_back, feed_gain_back, feed_shift_back, b_s, up_back, out_back, b_q = vectors
    b_s, b_q = b_s[: 2 * HEAD_DIM], b_q[:local]
    stacked = jnp.stack(shared_parts)
    ordered = jnp.stack([lax.dynamic_index_in_dim(stacked, me ^ j, 0, False) for j in range(parts)])
    g_s = jnp.swapaxes(ordered.reshape(parts, small_rows, width // LANES, LANES), 1, 2).reshape(-1, LANES)
    shared_back = g_s.astype(F32) * attention_gain[:, None] + attention_shift[:, None] * b_s[None, :]
    down_sum, up_sum = down_chain.finish(), up_chain.finish()
    query_back = payload[:local] * attention_gain[None, :]
    query_back = (query_back + b_q[:, None] * attention_shift[None, :]).T
    g_out = payload[local:].T
    up_back_matrix = up_sum.astype(F32) * feed_gain[:, None] + feed_shift[:, None] * up_back[None, :]
    return (
        mixed,
        tokens_back,
        gain_back,
        shift_back,
        feed_gain_back,
        feed_shift_back,
        query_back,
        b_q,
        shared_back,
        b_s,
        g_out,
        up_back_matrix,
        up_back,
        down_sum.astype(F32),
        out_back,
    )


def solution(mesh):
    return jax.shard_map(
        on_device,
        mesh=mesh,
        in_specs=(
            P(("batch", "tensor"), None),
            P("batch"),
            P(),
            P(("batch", "tensor"), None),
            P(),
            P(),
            P(),
            P(),
            P(None, "tensor"),
            P("tensor"),
            P(),
            P(),
            P(None, "tensor"),
            P(None, "tensor"),
            P("tensor"),
            P(None, "tensor"),
            P(),
        ),
        out_specs=(
            P(("batch", "tensor"), None),
            P(("batch", "tensor"), None),
            P(),
            P(),
            P(),
            P(),
            P(None, "tensor"),
            P("tensor"),
            P(),
            P(),
            P(None, "tensor"),
            P(None, "tensor"),
            P("tensor"),
            P(None, "tensor"),
            P(),
        ),
        check_vma=False,
    )
```
